32 devices in a mesh: snap: 4 (over x, core), param: 8 (over z, y).
Axes of the slice: x: 2, y: 2, z: 4, core: 2. Of those that a mesh axis runs over, the one named last changes fastest.
Arguments:
- snap_in: float32 [32, 64, 1344], P('snap', None, 'param'), may hold values from -6 to 6
- snap_qkv: float32 [32, 1344, 4032], P('snap', 'param'), may hold values from -6 to 6
- snap_proj: float32 [32, 1344, 1344], P('snap', 'param'), may hold values from -6 to 6
- snap_out: float32 [32, 1344, 64], P('snap', 'param'), may hold values from -48 to 48
- coeffs: float32 [32, 8], P('snap'), may hold values from -3 to 3
- latent: float32 [8, 64, 256], P('param'), may hold values from -6 to 6
- levels: int32 [8], P('param'), may hold values from 0 to 15
Outputs:
- denoised: float32 [8, 8, 64, 256], P('snap', 'param')
The draws below stay inside these ranges and needn't reach their ends.
All inputs are finite; a program needn't handle non-finite values.
Results may differ from the reference program's by a relative error of at most 0.012.
Values may be sent and summed in bfloat16 or wider, within the bound.
A program may use at most 192 MiB of HBM per device.

```python
import jax
import jax.numpy as jnp
from jax import lax

C = 1344
HEAD_DIM = 64
PROF = 8
SNAP_DEV = 8
NLEV = 16
SNAPS = 32
BATCH = 8
N_SNAP = 4
N_PARAM = 8


def draw_snap_out(key, part):
    base = jnp.clip(jax.random.normal(jax.random.fold_in(key, 11), (SNAPS, C, 64), jnp.float32), -6.0, 6.0)
    shift = jax.random.randint(jax.random.fold_in(key, 23), (), 0, N_PARAM)
    block = jnp.arange(C, dtype=jnp.int32) // (C // N_PARAM)
    column = jnp.arange(64, dtype=jnp.int32)
    paired = column[None, :] % N_PARAM == (block[:, None] + shift) % N_PARAM
    boost = jnp.where(paired, 8.0, 1.0).astype(jnp.float32)
    return base * boost[None, :, :]


def plant(drawn, key, least, top_value):
    place = [jax.random.randint(jax.random.fold_in(key, axis), (), 0, length) for axis, length in enumerate(drawn.shape)]
    longest = drawn.shape.index(max(drawn.shape))
    beside = place[:longest] + [(place[longest] + 1) % drawn.shape[longest]] + place[longest + 1:]
    return drawn.at[tuple(place)].set(least).at[tuple(beside)].set(top_value)


def raised(drawn, key, source, target, blocks, factor):
    def block_of(dim):
        return (jnp.arange(drawn.shape[dim]) // (drawn.shape[dim] // blocks)).reshape((-1,) + (1,) * (drawn.ndim - 1 - dim))

    first = jax.random.permutation(key, blocks)[block_of(target)]
    second = (block_of(target) + blocks // 2) % blocks
    return jnp.where((block_of(source) == first) | (block_of(source) == second), factor * drawn, drawn)


def shard_levels(rng, shape, pieces, least, top_value):
    loudness = 1.0
    for axis_at, blocks in pieces:
        heights = jax.random.uniform(jax.random.fold_in(jax.random.fold_in(rng, 6), axis_at), (blocks,), jnp.float32, least / len(pieces), top_value / len(pieces))
        loudness = loudness * jnp.repeat(jnp.exp(heights), shape[axis_at] // blocks).reshape((-1,) + (1,) * (len(shape) - 1 - axis_at))
    return loudness


def centred(key, extent, width, most, cuts=(), kind=jnp.bfloat16):
    entries = jax.random.normal(key, extent, jnp.float32) * width
    if len(cuts) > 0:
        entries = shard_levels(key, extent, cuts, -0.22, 0.18) * entries
    return jnp.clip(entries, min=-most, max=most).astype(kind)


def bell_draw_with(rng, dims, width, bound, split, heavy, kind=jnp.bfloat16):
    result = width * jax.random.normal(rng, dims, jnp.float32)
    if split:
        result = result * shard_levels(rng, dims, split, -0.22, 0.18)
    return jnp.clip(raised(result, jax.random.fold_in(rng, 3), *heavy), -bound, bound).astype(kind)


def setup_inputs(seed: int = 0) -> dict:
    key_list = jax.random.split(jax.random.key(seed), 8)
    return {
        "snap_in": centred(key_list[0], (SNAPS, 64, C), 1.0, 6.0, ((0, 4), (2, 8)), jnp.float32),
        "snap_qkv": bell_draw_with(key_list[1], (SNAPS, C, 3 * C), 1.0, 6.0, ((0, 4), (1, 8)), (1, 2, 8, 2.0), jnp.float32),
        "snap_proj": bell_draw_with(key_list[2], (SNAPS, C, C), 1.0, 6.0, ((0, 4), (1, 8)), (1, 2, 8, 2.0), jnp.float32),
        "snap_out": draw_snap_out(jax.random.fold_in(key_list[7], 71), 0),
        "coeffs": centred(key_list[4], (SNAPS, PROF), 0.5, 3.0, ((0, 4),), jnp.float32),
        "latent": centred(key_list[5], (BATCH, 64, 256), 1.0, 6.0, ((0, 8),), jnp.float32),
        "levels": plant(jax.random.randint(key_list[6], (BATCH,), 0, NLEV), jax.random.fold_in(key_list[6], 1), 0, NLEV - 1).astype(jnp.int32),
    }


EPS = 0.0001

def noise_scales(levels):
    step = levels.astype(jnp.float32) / (NLEV - 1)
    sigma = jnp.exp(jnp.log(0.2) + step * (jnp.log(5.0) - jnp.log(0.2)))
    square = sigma * sigma + 0.25
    return (1.0 / jnp.sqrt(square), 0.25 / square, 0.5 * sigma / jnp.sqrt(square))

def to_tokens(image):
    count = image.shape[0]
    parts = image.reshape(count, 16, 4, 16, 4, 4).transpose(0, 1, 3, 2, 4, 5)
    return parts.reshape(count, 256, 64)

def from_tokens(feature):
    count = feature.shape[0]
    parts = feature.reshape(count, 16, 16, 4, 4, 4).transpose(0, 1, 3, 2, 4, 5)
    return parts.reshape(count, 64, 256)

def column_unit(weights):
    norms = jnp.sqrt(lax.optimization_barrier(jnp.sum(weights * weights, axis=-2, keepdims=True)))
    return (weights / (EPS + norms)).astype(jnp.bfloat16)

def head_unit(values):
    scale = jnp.sqrt(lax.optimization_barrier(jnp.mean(values * values, axis=-1, keepdims=True)))
    return (values / (EPS + scale)).astype(jnp.bfloat16)

def forward(tokens, w_in, w_qkv, w_proj, w_out):
    rows = tokens.shape[0]
    count = rows // 256
    heads = C // HEAD_DIM
    hidden = jnp.dot(tokens, w_in, preferred_element_type=jnp.float32).astype(jnp.bfloat16)
    qkv = jnp.dot(hidden, w_qkv, preferred_element_type=jnp.float32)
    qkv = head_unit(qkv.reshape(count, 256, 3, heads, HEAD_DIM))
    query = qkv[:, :, 0].astype(jnp.float32)
    keys = qkv[:, :, 1].astype(jnp.float32)
    values = qkv[:, :, 2].astype(jnp.float32)
    scores = jnp.einsum('bqhd,bkhd->bhqk', query, keys) * (1.0 / jnp.sqrt(float(HEAD_DIM)))
    expo = jnp.exp(scores)
    weights = (expo / lax.optimization_barrier(jnp.sum(expo, axis=-1, keepdims=True))).astype(jnp.bfloat16)
    attended = jnp.einsum('bhqk,bkhd->bqhd', weights.astype(jnp.float32), values)
    attended = attended.astype(jnp.bfloat16).reshape(rows, C)
    projected = jnp.dot(attended, w_proj, preferred_element_type=jnp.float32)
    mixed = ((0.7 * hidden.astype(jnp.float32) + 0.3 * projected) / jnp.sqrt(0.58)).astype(jnp.bfloat16)
    return jnp.dot(mixed, w_out, preferred_element_type=jnp.float32)

def reference(snap_in, snap_qkv, snap_proj, snap_out, coeffs, latent, levels):
    groups = coeffs.reshape(N_SNAP, SNAP_DEV, PROF)

    def contract(snaps):
        total = None
        for group in range(N_SNAP):
            block = snaps[group * SNAP_DEV:(group + 1) * SNAP_DEV]
            part = jnp.einsum('sp,sij->pij', groups[group], block, precision=lax.Precision.HIGHEST)
            part = lax.optimization_barrier(part.astype(jnp.bfloat16)).astype(jnp.float32)
            total = part if total is None else total + part
        return total
    w_in = column_unit(contract(snap_in))
    w_qkv = column_unit(contract(snap_qkv))
    w_proj = column_unit(contract(snap_proj))
    w_out = column_unit(contract(snap_out))
    c_in, c_skip, c_out = noise_scales(levels)
    count = latent.shape[0]
    tokens = to_tokens(c_in[:, None, None] * latent).reshape(count * 256, 64).astype(jnp.bfloat16)

    def one_profile(weights):
        feature = forward(tokens, weights[0], weights[1], weights[2], weights[3])
        image = from_tokens(feature.reshape(count, 256, 64))
        return c_skip[:, None, None] * latent + c_out[:, None, None] * image
    return lax.map(one_profile, (w_in, w_qkv, w_proj, w_out))
```

```python
import jax
import jax.numpy as jnp
from jax import lax
from jax.sharding import PartitionSpec as P

HEAD_DIM = 64
PROF = 8
NLEV = 16


EPS = 0.0001


def noise_scales(levels):
    step = levels.astype(jnp.float32) / (NLEV - 1)
    sigma = jnp.exp(jnp.log(0.2) + step * (jnp.log(5.0) - jnp.log(0.2)))
    square = sigma * sigma + 0.25
    return (1.0 / jnp.sqrt(square), 0.25 / square, 0.5 * sigma / jnp.sqrt(square))


def to_tokens(image):
    count = image.shape[0]
    parts = image.reshape(count, 16, 4, 16, 4, 4).transpose(0, 1, 3, 2, 4, 5)
    return parts.reshape(count, 256, 64)


def from_tokens(feature):
    count = feature.shape[0]
    parts = feature.reshape(count, 16, 16, 4, 4, 4).transpose(0, 1, 3, 2, 4, 5)
    return parts.reshape(count, 64, 256)


def head_unit(values):
    scale = jnp.sqrt(jnp.mean(values * values, axis=-1, keepdims=True))
    return (values / (EPS + scale)).astype(jnp.bfloat16)


def contract(coeffs, snaps):
    return jnp.einsum("sp,sij->pij", coeffs, snaps, precision=lax.Precision.HIGHEST)


def squares(weights):
    return jnp.sum(weights * weights, axis=1)


def inverse_norms(sums):
    return 1.0 / (EPS + jnp.sqrt(sums))


def attend(tokens, mixed_qkv, mixed_out, skip_map):
    rows = tokens.shape[0]
    count = rows // 256
    width = mixed_out.shape[0]
    heads = width // HEAD_DIM
    qkv = jnp.dot(tokens, mixed_qkv, preferred_element_type=jnp.float32)
    qkv = head_unit(qkv.reshape(count, 256, 3, heads, HEAD_DIM))
    query = qkv[:, :, 0]
    keys = qkv[:, :, 1]
    values = qkv[:, :, 2]
    scores = jnp.einsum("bqhd,bkhd->bhqk", query, keys, preferred_element_type=jnp.float32)
    scores = scores * (1.0 / jnp.sqrt(float(HEAD_DIM)))
    expo = jnp.exp(scores)
    weights = (expo / jnp.sum(expo, axis=-1, keepdims=True)).astype(jnp.bfloat16)
    attended = jnp.einsum("bhqk,bkhd->bqhd", weights, values, preferred_element_type=jnp.float32)
    attended = attended.astype(jnp.bfloat16).reshape(rows, width)
    skip = jnp.dot(tokens.astype(jnp.float32), skip_map, precision=lax.Precision.HIGHEST)
    mapped = jnp.dot(attended, mixed_out, preferred_element_type=jnp.float32)
    return (0.7 * skip + 0.3 * mapped) / jnp.sqrt(0.58)


def prepare(latent, levels):
    c_in, c_skip, c_out = noise_scales(levels)
    count = latent.shape[0]
    tokens = to_tokens(c_in[:, None, None] * latent).reshape(count * 256, 64).astype(jnp.bfloat16)
    return (tokens, c_skip, c_out)


def finish(feature, latent, c_skip, c_out):
    count = latent.shape[0]
    image = from_tokens(feature.reshape(count, 256, 64))
    return c_skip[:, None, None] * latent + c_out[:, None, None] * image


def reduced(coeffs, snaps):
    part = contract(coeffs, snaps).astype(jnp.bfloat16)
    return lax.psum_scatter(part, "snap", scatter_dimension=0, tiled=True).astype(jnp.float32)


def rows_product(left, right):
    return jnp.einsum("pfr,prc->pfc", left, right.astype(jnp.bfloat16), preferred_element_type=jnp.float32)


def shards(snap_in, snap_qkv, snap_proj, snap_out, coeffs, latent, levels):
    owned = PROF // lax.axis_size("snap")
    prof_in = reduced(coeffs, snap_in)
    prof_out = reduced(coeffs, snap_out)
    prof_proj = reduced(coeffs, snap_proj)
    prof_qkv = reduced(coeffs, snap_qkv)
    unit_in = (prof_in * inverse_norms(squares(prof_in))[:, None, :]).astype(jnp.bfloat16)
    full_out = lax.all_gather(prof_out, "param", axis=1, tiled=True)
    unit_out = full_out * inverse_norms(squares(full_out))[:, None, :]
    part_map = rows_product(unit_in, prof_qkv)
    part_skip = jnp.einsum(
        "pfr,prc->pfc", unit_in.astype(jnp.float32), prof_out, precision=lax.Precision.HIGHEST
    )
    sums_qkv, sums_proj, qkv_map, skip_map = lax.psum(
        (squares(prof_qkv), squares(prof_proj), part_map, part_skip), "param"
    )
    qkv_map = (qkv_map * inverse_norms(sums_qkv)[:, None, :]).astype(jnp.bfloat16)
    skip_map = skip_map * inverse_norms(squares(full_out))[:, None, :]
    scaled_out = (unit_out * inverse_norms(sums_proj)[:, :, None]).astype(jnp.bfloat16)
    own_rows = jnp.einsum(
        "prc,pcf->prf", prof_proj.astype(jnp.bfloat16), scaled_out, preferred_element_type=jnp.float32
    ).astype(jnp.bfloat16)
    out_map = lax.all_gather(own_rows, "param", axis=1, tiled=True)
    tokens, c_skip, c_out = prepare(latent, levels)
    results = []
    for profile in range(owned):
        feature = attend(tokens, qkv_map[profile], out_map[profile], skip_map[profile])
        results.append(finish(feature, latent, c_skip, c_out))
    return jnp.stack(results)


def solution(mesh):
    in_specs = (
        P("snap", None, "param"),
        P("snap", "param", None),
        P("snap", "param", None),
        P("snap", "param", None),
        P("snap", None),
        P("param", None, None),
        P("param"),
    )
    out_specs = P("snap", "param", None, None)
    return jax.shard_map(shards, mesh=mesh, in_specs=in_specs, out_specs=out_specs, check_vma=False)
```

```python
import functools

import jax
import jax.numpy as jnp
from jax import lax
from jax.experimental import pallas as pl
from jax.experimental.pallas import tpu as pltpu
from jax.sharding import PartitionSpec as P

HEAD_DIM = 64
PROF = 8
NLEV = 16


EPS = 0.0001


def noise_scales(levels):
    step = levels.astype(jnp.float32) / (NLEV - 1)
    sigma = jnp.exp(jnp.log(0.2) + step * (jnp.log(5.0) - jnp.log(0.2)))
    square = sigma * sigma + 0.25
    return (1.0 / jnp.sqrt(square), 0.25 / square, 0.5 * sigma / jnp.sqrt(square))


def to_tokens(image):
    count = image.shape[0]
    parts = image.reshape(count, 16, 4, 16, 4, 4).transpose(0, 1, 3, 2, 4, 5)
    return parts.reshape(count, 256, 64)


def from_tokens(feature):
    count = feature.shape[0]
    parts = feature.reshape(count, 16, 16, 4, 4, 4).transpose(0, 1, 3, 2, 4, 5)
    return parts.reshape(count, 64, 256)


def head_unit(values):
    scale = jnp.sqrt(jnp.mean(values * values, axis=-1, keepdims=True))
    return (values / (EPS + scale)).astype(jnp.bfloat16)


def inverse_norms(sums):
    return 1.0 / (EPS + jnp.sqrt(sums))


def attend(tokens, mixed_qkv, mixed_out, skip_map):
    rows = tokens.shape[0]
    count = rows // 256
    width = mixed_out.shape[0]
    heads = width // HEAD_DIM
    qkv = jnp.dot(tokens, mixed_qkv, preferred_element_type=jnp.float32)
    qkv = head_unit(qkv.reshape(count, 256, 3, heads, HEAD_DIM))
    query = qkv[:, :, 0]
    keys = qkv[:, :, 1]
    values = qkv[:, :, 2]
    scores = jnp.einsum("bqhd,bkhd->bhqk", query, keys, preferred_element_type=jnp.float32)
    scores = scores * (1.0 / jnp.sqrt(float(HEAD_DIM)))
    expo = jnp.exp(scores)
    weights = (expo / jnp.sum(expo, axis=-1, keepdims=True)).astype(jnp.bfloat16)
    attended = jnp.einsum("bhqk,bkhd->bqhd", weights, values, preferred_element_type=jnp.float32)
    attended = attended.astype(jnp.bfloat16).reshape(rows, width)
    skip = jnp.dot(tokens.astype(jnp.float32), skip_map, precision=lax.Precision.HIGHEST)
    mapped = jnp.dot(attended, mixed_out, preferred_element_type=jnp.float32)
    return (0.7 * skip + 0.3 * mapped) / jnp.sqrt(0.58)


def prepare(latent, levels):
    c_in, c_skip, c_out = noise_scales(levels)
    count = latent.shape[0]
    tokens = to_tokens(c_in[:, None, None] * latent).reshape(count * 256, 64).astype(jnp.bfloat16)
    return (tokens, c_skip, c_out)


def finish(feature, latent, c_skip, c_out):
    count = latent.shape[0]
    image = from_tokens(feature.reshape(count, 256, 64))
    return c_skip[:, None, None] * latent + c_out[:, None, None] * image


LANES = 128
SUB = 8
PIECE = 256


def cut(width, pieces):
    tiles = width // LANES
    sizes = [tiles // pieces + (1 if i < tiles % pieces else 0) for i in range(pieces)]
    return [size * LANES for size in sizes if size]


def exchange_kernel(
    cuts, proj_count, n, groups, real,
    coeffs, aux, proj, qkv,
    *refs,
):
    total = len(cuts)
    maps = total - proj_count
    pos = 0

    def take(count):
        nonlocal pos
        pos += count
        return refs[pos - count:pos]

    k_out = take(maps)
    (m_out, skip_out) = take(2)
    (feed,) = take(1)
    away, keep, near, over, far = (take(total) for _ in range(5))
    g_send, g_recv, q_send, q_recv = (take(maps) for _ in range(4))
    (aux_all, proj_w, proj_sq, proj_sq_in, unit_rows) = take(5)
    (feed_sem, near_sems, far_sems, map_sems, aux_sems, sq_sems, m_sems) = take(7)

    rows = groups * 2 * SUB
    snap = lax.axis_index("snap")
    me = lax.axis_index("param")
    core = lax.rem(snap, 2)
    sibling = snap + 1 - 2 * core
    across = lax.rem(snap + 2, 4)

    def peer(step):
        return {"snap": snap, "param": lax.rem(me + step, n)}

    barrier = pltpu.get_barrier_semaphore()
    for other in (sibling, across):
        pl.semaphore_signal(
            barrier, inc=1, device_id={"snap": other, "param": me},
            device_id_type=pl.DeviceIdType.MESH,
        )

    def greet(step, carry):
        pl.semaphore_signal(
            barrier, inc=1, device_id=peer(step), device_id_type=pl.DeviceIdType.MESH
        )
        return carry

    lax.fori_loop(1, n, greet, 0)

    sources = []
    offset = 0
    sources.append((aux, 0))
    for index in range(1, total):
        if index <= proj_count:
            sources.append((proj, offset))
        else:
            sources.append((qkv, offset))
        offset += cuts[index]
        if index == proj_count:
            offset = 0

    def fetch(index):
        source, start = sources[index]
        slot = index % 2
        return pltpu.make_async_copy(
            source.at[:, :, start:start + cuts[index]],
            feed.at[slot, :, :, 0:cuts[index]],
            feed_sem.at[slot],
        )

    def remote(source, target, sems, at, device):
        return pltpu.make_async_remote_copy(
            src_ref=source, dst_ref=target, send_sem=sems.at[(0,) + at], recv_sem=sems.at[(1,) + at],
            device_id=device, device_id_type=pl.DeviceIdType.MESH,
        )

    def near_copy(index):
        return remote(away[index], near[index], near_sems, (index,), {"snap": sibling, "param": me})

    def far_copy(index):
        return remote(over[index], far[index], far_sems, (index,), {"snap": across, "param": me})

    def each_peer(act):
        def body(step, carry):
            act(step)
            return carry

        lax.fori_loop(1, n, body, 0)

    def map_copies(index, step):
        goal = lax.rem(me + step, n)
        half = (goal * 2) // n
        return (
            remote(g_send[index].at[goal], g_recv[index].at[step], map_sems, (index, 0, step), peer(step)),
            remote(q_send[index].at[half], q_recv[index].at[step], map_sems, (index, 1, step), peer(step)),
        )

    def map_spread(index, step):
        return remote(
            k_out[index].at[me], k_out[index].at[me], map_sems, (index, 2, step), peer(step)
        )

    def aux_copy(step):
        return remote(aux_all.at[me], aux_all.at[me], aux_sems, (step,), peer(step))

    def sq_copy(step):
        return remote(proj_sq, proj_sq_in.at[step], sq_sems, (step,), peer(step))

    def m_copy(step):
        return remote(m_out.at[me], m_out.at[me], m_sems, (step,), peer(step))

    def contract(index):
        width = cuts[index]
        slot = index % 2

        def body(group, carry):
            at = pl.ds(pl.multiple_of(group * SUB, SUB), SUB)
            to = pl.ds(pl.multiple_of(group * 2 * SUB, 2 * SUB), 2 * SUB)
            for start in range(0, width, PIECE):
                lanes = slice(start, min(start + PIECE, width))
                snaps = [feed[slot, s, at, lanes] for s in range(feed.shape[1])]
                for pair in range(4):
                    both = []
                    for column in (2 * pair, 2 * pair + 1):
                        value = coeffs[0, column] * snaps[0]
                        for s in range(1, len(snaps)):
                            value = value + coeffs[s, column] * snaps[s]
                        both.append(value)
                    packed = jnp.concatenate(both, axis=0).astype(jnp.bfloat16)
                    if pair < 2:
                        keep[index][pair, to, lanes] = packed
                    else:
                        away[index][pair - 2, to, lanes] = packed
            return carry

        lax.fori_loop(0, groups, body, 0)

    def pass_on(index):
        near_copy(index).wait_recv()

        def body(group, carry):
            to = pl.ds(pl.multiple_of(group * 2 * SUB, 2 * SUB), 2 * SUB)
            own = keep[index][1, to, :].astype(jnp.float32) + near[index][1, to, :].astype(jnp.float32)
            over[index][to, :] = own.astype(jnp.bfloat16)
            return carry

        lax.fori_loop(0, groups, body, 0)
        far_copy(index).start()

    def finish_sum(index):
        far_copy(index).wait_recv()

        def body(group, squares):
            to = pl.ds(pl.multiple_of(group * 2 * SUB, 2 * SUB), 2 * SUB)
            own = keep[index][0, to, :].astype(jnp.float32) + near[index][0, to, :].astype(jnp.float32)
            own = own + far[index][to, :].astype(jnp.float32)
            keep[index][0, to, :] = own.astype(jnp.bfloat16)
            return squares + own * own

        start = jnp.zeros((2 * SUB, cuts[index]), jnp.float32)
        squares = lax.fori_loop(0, groups, body, start)
        return (
            jnp.sum(squares[:SUB], axis=0, keepdims=True),
            jnp.sum(squares[SUB:], axis=0, keepdims=True),
        )

    def send_map(index, weights, squares):
        product = lax.dot_general(
            unit_rows[...], weights, (((0,), (0,)), ((), ())), preferred_element_type=jnp.float32
        ).astype(jnp.bfloat16)
        share = g_send[index].shape[1]
        for goal in range(n):
            g_send[index][goal] = product[goal * share:(goal + 1) * share]
        q_send[index][0] = squares[0]
        q_send[index][1] = squares[1]

        def act(step):
            for copy in map_copies(index, step):
                copy.start()

        each_peer(act)

    def finish_map(index):
        def act(step):
            for copy in map_copies(index, step):
                copy.wait_recv()

        each_peer(act)
        product = g_send[index][me].astype(jnp.float32)
        squares = q_send[index][(me * 2) // n]
        for step in range(1, n):
            product = product + g_recv[index][step].astype(jnp.float32)
            squares = squares + q_recv[index][step]
        scaled = product * (1.0 / (EPS + jnp.sqrt(squares)))
        k_out[index][me] = scaled.astype(jnp.bfloat16)
        each_peer(lambda step: map_spread(index, step).start())

    def unit_in_rows(values):
        lane = lax.broadcasted_iota(jnp.int32, values.shape, 1)
        left = jnp.where(lane < LANES // 2, values, 0.0)
        norm = jnp.sqrt(jnp.sum(left * left, axis=1, keepdims=True))
        return left / (EPS + norm)

    def start_aux():
        squares = finish_sum(0)
        own = keep[0][0, :, 0:LANES]
        aux_all[me] = own
        each_peer(lambda step: aux_copy(step).start())
        unit = unit_in_rows(own.astype(jnp.float32))
        unit = unit + pltpu.roll(unit, LANES // 2, 1)
        row = lax.broadcasted_iota(jnp.int32, unit.shape, 0)
        lane = lax.broadcasted_iota(jnp.int32, unit.shape, 1)
        same = lax.rem(row, 2 * SUB) // SUB == lane // (LANES // 2)
        unit_rows[...] = jnp.where(same, unit, 0.0).astype(jnp.bfloat16)
        rest = keep[0][0, :, LANES:]
        proj_width = proj_w.shape[1] - LANES
        proj_w[:, proj_width:] = jnp.where(lane < LANES // 2, rest, jnp.zeros_like(rest))
        first = lax.broadcasted_iota(jnp.int32, (1, LANES), 1) < LANES // 2
        for profile in range(2):
            proj_sq[profile, :, proj_width:] = jnp.where(first, squares[profile][:, LANES:], 0.0)
        send_map(0, rest, [square[:, LANES:] for square in squares])

    def start_proj(index, offset):
        squares = finish_sum(index)
        proj_w[:, offset:offset + cuts[index]] = keep[index][0]
        for profile in range(2):
            proj_sq[profile, :, offset:offset + cuts[index]] = squares[profile]

    def out_maps():
        each_peer(lambda step: aux_copy(step).wait_recv())
        each_peer(lambda step: sq_copy(step).wait_recv())
        sums = proj_sq[...]
        for step in range(1, n):
            sums = sums + proj_sq_in[step]
        inverse = 1.0 / (EPS + jnp.sqrt(sums))
        values = aux_all[...].astype(jnp.float32).reshape(n * groups, 2 * SUB, LANES)
        results = []
        depth = n * real
        for profile in range(2):
            own = values[:, profile * SUB:(profile + 1) * SUB].reshape(n * groups * SUB, LANES)
            if real < groups * SUB:
                starts = range(0, n * groups * SUB, groups * SUB)
                own = jnp.concatenate([own[start:start + real] for start in starts], axis=0)
            norm = jnp.sqrt(jnp.sum(own * own, axis=0, keepdims=True))
            unit_out = (own / (EPS + norm)).astype(jnp.bfloat16)
            unit_in = unit_in_rows(own).astype(jnp.bfloat16)
            skip_out[profile] = lax.dot_general(
                unit_in, unit_out, (((0,), (0,)), ((), ())), preferred_element_type=jnp.float32
            )
            spare = jnp.zeros((proj_w.shape[1] - depth, LANES), jnp.bfloat16)
            tall = jnp.concatenate([unit_out, spare], axis=0)
            weights = (proj_w[...].astype(jnp.float32) * inverse[profile]).astype(jnp.bfloat16)
            results.append(jnp.dot(weights, tall, preferred_element_type=jnp.float32))
        row = lax.broadcasted_iota(jnp.int32, results[0].shape, 0)
        chosen = jnp.where(lax.rem(row, 2 * SUB) < SUB, results[0], results[1])
        m_out[me] = chosen.astype(jnp.bfloat16)
        each_peer(lambda step: m_copy(step).start())

    fetch(0).start()
    for index in range(total):
        if index + 1 < total:
            fetch(index + 1).start()
        fetch(index).wait()
        contract(index)
        if index == 0:
            pl.semaphore_wait(barrier, n + 1)
        near_copy(index).start()
        if index >= 1:
            pass_on(index - 1)
    pass_on(total - 1)

    start_aux()
    offset = 0
    for index in range(1, proj_count + 1):
        start_proj(index, offset)
        offset += cuts[index]
    each_peer(lambda step: sq_copy(step).start())
    finish_map(0)
    for index in range(1, maps):
        chunk = index + proj_count
        squares = finish_sum(chunk)
        send_map(index, keep[chunk][0], squares)
        if index == 1:
            out_maps()
        if index >= 2:
            finish_map(index - 1)
    finish_map(maps - 1)

    for index in range(maps):
        each_peer(lambda step: map_spread(index, step).wait_recv())
    each_peer(lambda step: m_copy(step).wait_recv())
    for index in range(total):
        near_copy(index).wait_send()
        far_copy(index).wait_send()

    def drain(step):
        for index in range(maps):
            for copy in map_copies(index, step):
                copy.wait_send()
            map_spread(index, step).wait_send()
        aux_copy(step).wait_send()
        sq_copy(step).wait_send()
        m_copy(step).wait_send()

    each_peer(drain)


def exchange_call(coeffs, aux, proj, qkv, n, real, main_proj, main_qkv):
    snaps, rows, _ = aux.shape
    groups = rows // SUB
    proj_cuts = cut(main_proj, 2)
    cuts = [aux.shape[2]] + proj_cuts + cut(main_qkv, 5)
    total = len(cuts)
    map_cuts = [LANES] + cuts[1 + len(proj_cuts):]
    maps = len(map_cuts)
    both = 2 * rows
    share = LANES // n
    proj_wide = main_proj + LANES
    kind, wide = jnp.bfloat16, jnp.float32
    shapes = [jax.ShapeDtypeStruct((n, share, width), kind) for width in map_cuts]
    shapes += [
        jax.ShapeDtypeStruct((n, both, LANES), kind),
        jax.ShapeDtypeStruct((2, LANES, LANES), wide),
    ]
    scratch = [pltpu.VMEM((2, snaps, rows, max(cuts)), wide)]
    for lead in ((2,), (2,), (2,), (), ()):
        scratch += [pltpu.VMEM(lead + (both, width), kind) for width in cuts]
    scratch += [pltpu.VMEM((n, share, width), kind) for width in map_cuts]
    scratch += [pltpu.VMEM((n, share, width), kind) for width in map_cuts]
    scratch += [pltpu.VMEM((2, 1, width), wide) for width in map_cuts]
    scratch += [pltpu.VMEM((n, 1, width), wide) for width in map_cuts]
    scratch += [
        pltpu.VMEM((n, both, LANES), kind),
        pltpu.VMEM((both, proj_wide), kind),
        pltpu.VMEM((2, 1, proj_wide), wide),
        pltpu.VMEM((n, 2, 1, proj_wide), wide),
        pltpu.VMEM((both, LANES), kind),
        pltpu.SemaphoreType.DMA((2,)),
        pltpu.SemaphoreType.DMA((2, total)),
        pltpu.SemaphoreType.DMA((2, total)),
        pltpu.SemaphoreType.DMA((2, maps, 3, n)),
        pltpu.SemaphoreType.DMA((2, n)),
        pltpu.SemaphoreType.DMA((2, n)),
        pltpu.SemaphoreType.DMA((2, n)),
    ]
    hbm = pl.BlockSpec(memory_space=pl.ANY)
    return pl.pallas_call(
        functools.partial(exchange_kernel, tuple(cuts), len(proj_cuts), n, groups, real),
        out_shape=shapes,
        in_specs=[pl.BlockSpec(memory_space=pltpu.SMEM), hbm, hbm, hbm],
        out_specs=[pl.BlockSpec(memory_space=pltpu.VMEM)] * len(shapes),
        scratch_shapes=scratch,
        compiler_params=pltpu.CompilerParams(
            collective_id=0, has_side_effects=True, vmem_limit_bytes=60 * 2**20
        ),
    )(coeffs, aux, proj, qkv)


def shards(snap_in, snap_qkv, snap_proj, snap_out, coeffs, latent, levels):
    owned = PROF // lax.axis_size("snap")
    n = lax.axis_size("param")
    snap = lax.axis_index("snap")
    width = snap_proj.shape[2]
    rows = snap_qkv.shape[1]
    main_proj = width // LANES * LANES
    main_qkv = snap_qkv.shape[2] // LANES * LANES
    aux = jnp.concatenate(
        [snap_in.transpose(0, 2, 1), snap_out, snap_proj[:, :, main_proj:], snap_qkv[:, :, main_qkv:]],
        axis=2,
    )
    main = [snap_proj, snap_qkv]
    spare = -rows % SUB
    if spare:
        aux, *main = [jnp.pad(x, ((0, 0), (0, spare), (0, 0))) for x in [aux] + main]
    order = jnp.stack([snap, (snap + 2) % 4, snap + 1 - 2 * (snap % 2), (snap + 3 - 2 * (snap % 2)) % 4])
    columns = jnp.take(coeffs.reshape(-1, 4, owned), order, axis=1).reshape(coeffs.shape)
    *maps, out_map, skip_map = exchange_call(columns, aux, main[0], main[1], n, rows, main_proj, main_qkv)
    maps = [part.reshape(owned, -1, part.shape[2]) for part in maps]
    half = LANES // 2
    qkv_map = jnp.concatenate(maps[1:] + [maps[0][:, :, half:]], axis=2)
    out_map = out_map.reshape(n, -1, owned, SUB, LANES)[..., half:]
    out_map = out_map.transpose(2, 0, 1, 3, 4).reshape(owned, n, -1, half)[:, :, :rows]
    out_map = out_map.reshape(owned, n * rows, half)
    skip_map = skip_map[:, :half, half:]
    tokens, c_skip, c_out = prepare(latent, levels)
    results = []
    for profile in range(owned):
        feature = attend(tokens, qkv_map[profile], out_map[profile], skip_map[profile])
        results.append(finish(feature, latent, c_skip, c_out))
    return jnp.stack(results)


def solution(mesh):
    in_specs = (
        P("snap", None, "param"),
        P("snap", "param", None),
        P("snap", "param", None),
        P("snap", "param", None),
        P("snap", None),
        P("param", None, None),
        P("param"),
    )
    out_specs = P("snap", "param", None, None)
    return jax.shard_map(shards, mesh=mesh, in_specs=in_specs, out_specs=out_specs, check_vma=False)
```

```python
import functools

import jax
import jax.numpy as jnp
from jax import lax
from jax.experimental import pallas as pl
from jax.experimental.pallas import tpu as pltpu
from jax.sharding import PartitionSpec as P

HEAD_DIM = 64
PROF = 8
NLEV = 16


EPS = 0.0001


def noise_scales(levels):
    step = levels.astype(jnp.float32) / (NLEV - 1)
    sigma = jnp.exp(jnp.log(0.2) + step * (jnp.log(5.0) - jnp.log(0.2)))
    square = sigma * sigma + 0.25
    return (1.0 / jnp.sqrt(square), 0.25 / square, 0.5 * sigma / jnp.sqrt(square))


def to_tokens(image):
    count = image.shape[0]
    parts = image.reshape(count, 16, 4, 16, 4, 4).transpose(0, 1, 3, 2, 4, 5)
    return parts.reshape(count, 256, 64)


def from_tokens(feature):
    count = feature.shape[0]
    parts = feature.reshape(count, 16, 16, 4, 4, 4).transpose(0, 1, 3, 2, 4, 5)
    return parts.reshape(count, 64, 256)


def head_unit(values):
    scale = jnp.sqrt(jnp.mean(values * values, axis=-1, keepdims=True))
    return (values / (EPS + scale)).astype(jnp.bfloat16)


def inverse_norms(sums):
    return 1.0 / (EPS + jnp.sqrt(sums))


def attend(tokens, mixed_qkv, mixed_out, skip_map):
    rows = tokens.shape[0]
    count = rows // 256
    width = mixed_out.shape[0]
    heads = width // HEAD_DIM
    qkv = jnp.dot(tokens, mixed_qkv, preferred_element_type=jnp.float32)
    qkv = head_unit(qkv.reshape(count, 256, 3, heads, HEAD_DIM))
    query = qkv[:, :, 0]
    keys = qkv[:, :, 1]
    values = qkv[:, :, 2]
    scores = jnp.einsum("bqhd,bkhd->bhqk", query, keys, preferred_element_type=jnp.float32)
    scores = scores * (1.0 / jnp.sqrt(float(HEAD_DIM)))
    expo = jnp.exp(scores)
    weights = (expo / jnp.sum(expo, axis=-1, keepdims=True)).astype(jnp.bfloat16)
    attended = jnp.einsum("bhqk,bkhd->bqhd", weights, values, preferred_element_type=jnp.float32)
    attended = attended.astype(jnp.bfloat16).reshape(rows, width)
    skip = jnp.dot(tokens.astype(jnp.float32), skip_map, precision=lax.Precision.HIGHEST)
    mapped = jnp.dot(attended, mixed_out, preferred_element_type=jnp.float32)
    return (0.7 * skip + 0.3 * mapped) / jnp.sqrt(0.58)


def prepare(latent, levels):
    c_in, c_skip, c_out = noise_scales(levels)
    count = latent.shape[0]
    tokens = to_tokens(c_in[:, None, None] * latent).reshape(count * 256, 64).astype(jnp.bfloat16)
    return (tokens, c_skip, c_out)


def finish(feature, latent, c_skip, c_out):
    count = latent.shape[0]
    image = from_tokens(feature.reshape(count, 256, 64))
    return c_skip[:, None, None] * latent + c_out[:, None, None] * image


LANES = 128
SUB = 8
PIECE = 256


def cut(width, pieces):
    tiles = width // LANES
    sizes = [tiles // pieces + (1 if i < tiles % pieces else 0) for i in range(pieces)]
    return [size * LANES for size in sizes if size]


def head_plan(pairs):
    sizes = cut(pairs * LANES, 5)
    sizes = [size // LANES for size in sizes]
    if len(sizes) > 2 and sizes[-1] > 1:
        sizes[0] += 1
        sizes[-1] -= 1
    plan = []
    first = 0
    for size in sizes:
        last = first + size
        key_first = first + 1 if first else 0
        plan.append(
            (
                (first, last),
                (pairs + key_first, pairs + last + 1),
                (2 * pairs + 1 + first, 2 * pairs + 1 + last),
            )
        )
        first = last
    return tuple(plan)


def tile_places(plan):
    places = {}
    for index, parts in enumerate(plan):
        lane = 0
        for first, last in parts:
            for tile in range(first, last):
                places[tile] = (index + 1, lane)
                lane += LANES
    places[len(places)] = (0, 0)
    return places


def exchange_kernel(
    plan, cuts, proj_count, n, groups, real, fused,
    coeffs, aux, proj, qkv, tokens,
    *refs,
):
    total = len(cuts)
    maps = total - proj_count
    places = tile_places(plan)
    pos = 0

    def take(count):
        nonlocal pos
        pos += count
        return refs[pos - count:pos]

    k_out = take(maps)
    (m_out, skip_out, feature) = take(3)
    (feed,) = take(1)
    away, keep, near, over, far = (take(total) for _ in range(5))
    g_send, g_recv, q_send, q_recv = (take(maps) for _ in range(4))
    (aux_all, proj_w, proj_sq, proj_sq_in, unit_rows, out_rows) = take(6)
    (feed_sem, near_sems, far_sems, map_sems, aux_sems, sq_sems, m_sems) = take(7)

    rows = groups * 2 * SUB
    snap = lax.axis_index("snap")
    me = lax.axis_index("param")
    core = lax.rem(snap, 2)
    sibling = snap + 1 - 2 * core
    across = lax.rem(snap + 2, 4)

    def peer(step):
        return {"snap": snap, "param": lax.rem(me + step, n)}

    barrier = pltpu.get_barrier_semaphore()
    for other in (sibling, across):
        pl.semaphore_signal(
            barrier, inc=1, device_id={"snap": other, "param": me},
            device_id_type=pl.DeviceIdType.MESH,
        )

    def greet(step, carry):
        pl.semaphore_signal(
            barrier, inc=1, device_id=peer(step), device_id_type=pl.DeviceIdType.MESH
        )
        return carry

    lax.fori_loop(1, n, greet, 0)

    starts = [[(0, cuts[0])]]
    for index in range(proj_count):
        starts.append([(sum(cuts[1:1 + index]), cuts[1 + index])])
    for parts in plan:
        starts.append([(first * LANES, (last - first) * LANES) for first, last in parts])
    sources = [aux] + [proj] * proj_count + [qkv] * len(plan)

    def fetches(index):
        slot = index % 2
        copies = []
        at = 0
        for which, (start, width) in enumerate(starts[index]):
            copies.append(
                pltpu.make_async_copy(
                    sources[index].at[:, :, start:start + width],
                    feed.at[slot, :, :, at:at + width],
                    feed_sem.at[slot, which],
                )
            )
            at += width
        return copies

    def remote(source, target, sems, at, device):
        return pltpu.make_async_remote_copy(
            src_ref=source, dst_ref=target, send_sem=sems.at[(0,) + at], recv_sem=sems.at[(1,) + at],
            device_id=device, device_id_type=pl.DeviceIdType.MESH,
        )

    def near_copy(index):
        return remote(away[index], near[index], near_sems, (index,), {"snap": sibling, "param": me})

    def far_copy(index):
        return remote(over[index], far[index], far_sems, (index,), {"snap": across, "param": me})

    def each_peer(act):
        def body(step, carry):
            act(step)
            return carry

        lax.fori_loop(1, n, body, 0)

    def map_copies(index, step):
        goal = lax.rem(me + step, n)
        half = (goal * 2) // n
        return (
            remote(g_send[index].at[goal], g_recv[index].at[step], map_sems, (index, 0, step), peer(step)),
            remote(q_send[index].at[half], q_recv[index].at[step], map_sems, (index, 1, step), peer(step)),
        )

    def map_spread(index, step):
        return remote(
            k_out[index].at[me], k_out[index].at[me], map_sems, (index, 2, step), peer(step)
        )

    def aux_copy(step):
        return remote(aux_all.at[me], aux_all.at[me], aux_sems, (step,), peer(step))

    def sq_copy(step):
        return remote(proj_sq, proj_sq_in.at[step], sq_sems, (step,), peer(step))

    def m_copy(step):
        return remote(m_out.at[me], m_out.at[me], m_sems, (step,), peer(step))

    pairs = (snap, across, sibling, lax.rem(sibling + 2, 4))

    def contract(index):
        width = cuts[index]
        slot = index % 2

        def body(group, carry):
            at = pl.ds(pl.multiple_of(group * SUB, SUB), SUB)
            to = pl.ds(pl.multiple_of(group * 2 * SUB, 2 * SUB), 2 * SUB)
            for start in range(0, width, PIECE):
                lanes = slice(start, min(start + PIECE, width))
                snaps = [feed[slot, s, at, lanes] for s in range(feed.shape[1])]
                for pair in range(4):
                    both = []
                    for column in (2 * pairs[pair], 2 * pairs[pair] + 1):
                        value = coeffs[0, column] * snaps[0]
                        for s in range(1, len(snaps)):
                            value = value + coeffs[s, column] * snaps[s]
                        both.append(value)
                    packed = jnp.concatenate(both, axis=0).astype(jnp.bfloat16)
                    if pair < 2:
                        keep[index][pair, to, lanes] = packed
                    else:
                        away[index][pair - 2, to, lanes] = packed
            return carry

        lax.fori_loop(0, groups, body, 0)

    def pass_on(index):
        near_copy(index).wait_recv()

        def body(group, carry):
            to = pl.ds(pl.multiple_of(group * 2 * SUB, 2 * SUB), 2 * SUB)
            own = keep[index][1, to, :].astype(jnp.float32) + near[index][1, to, :].astype(jnp.float32)
            over[index][to, :] = own.astype(jnp.bfloat16)
            return carry

        lax.fori_loop(0, groups, body, 0)
        far_copy(index).start()

    def finish_sum(index):
        far_copy(index).wait_recv()

        def body(group, squares):
            to = pl.ds(pl.multiple_of(group * 2 * SUB, 2 * SUB), 2 * SUB)
            own = keep[index][0, to, :].astype(jnp.float32) + near[index][0, to, :].astype(jnp.float32)
            own = own + far[index][to, :].astype(jnp.float32)
            keep[index][0, to, :] = own.astype(jnp.bfloat16)
            return squares + own * own

        start = jnp.zeros((2 * SUB, cuts[index]), jnp.float32)
        squares = lax.fori_loop(0, groups, body, start)
        return (
            jnp.sum(squares[:SUB], axis=0, keepdims=True),
            jnp.sum(squares[SUB:], axis=0, keepdims=True),
        )

    def send_map(index, weights, squares):
        product = lax.dot_general(
            unit_rows[...], weights, (((0,), (0,)), ((), ())), preferred_element_type=jnp.float32
        ).astype(jnp.bfloat16)
        share = g_send[index].shape[1]
        for goal in range(n):
            g_send[index][goal] = product[goal * share:(goal + 1) * share]
        q_send[index][0] = squares[0]
        q_send[index][1] = squares[1]

        def act(step):
            for copy in map_copies(index, step):
                copy.start()

        each_peer(act)

    def finish_map(index):
        def act(step):
            for copy in map_copies(index, step):
                copy.wait_recv()

        each_peer(act)
        product = g_send[index][me].astype(jnp.float32)
        squares = q_send[index][(me * 2) // n]
        for step in range(1, n):
            product = product + g_recv[index][step].astype(jnp.float32)
            squares = squares + q_recv[index][step]
        scaled = product * (1.0 / (EPS + jnp.sqrt(squares)))
        k_out[index][me] = scaled.astype(jnp.bfloat16)
        each_peer(lambda step: map_spread(index, step).start())

    def unit_in_rows(values):
        lane = lax.broadcasted_iota(jnp.int32, values.shape, 1)
        left = jnp.where(lane < LANES // 2, values, 0.0)
        norm = jnp.sqrt(jnp.sum(left * left, axis=1, keepdims=True))
        return left / (EPS + norm)

    def start_aux():
        squares = finish_sum(0)
        own = keep[0][0, :, 0:LANES]
        aux_all[me] = own
        each_peer(lambda step: aux_copy(step).start())
        unit = unit_in_rows(own.astype(jnp.float32))
        unit = unit + pltpu.roll(unit, LANES // 2, 1)
        row = lax.broadcasted_iota(jnp.int32, unit.shape, 0)
        lane = lax.broadcasted_iota(jnp.int32, unit.shape, 1)
        same = lax.rem(row, 2 * SUB) // SUB == lane // (LANES // 2)
        unit_rows[...] = jnp.where(same, unit, 0.0).astype(jnp.bfloat16)
        rest = keep[0][0, :, LANES:]
        proj_width = proj_w.shape[1] - LANES
        proj_w[:, proj_width:] = jnp.where(lane < LANES // 2, rest, jnp.zeros_like(rest))
        first = lax.broadcasted_iota(jnp.int32, (1, LANES), 1) < LANES // 2
        for profile in range(2):
            proj_sq[profile, :, proj_width:] = jnp.where(first, squares[profile][:, LANES:], 0.0)
        send_map(0, rest, [square[:, LANES:] for square in squares])

    def start_proj(index, offset):
        squares = finish_sum(index)
        proj_w[:, offset:offset + cuts[index]] = keep[index][0]
        for profile in range(2):
            proj_sq[profile, :, offset:offset + cuts[index]] = squares[profile]

    def out_maps():
        each_peer(lambda step: aux_copy(step).wait_recv())
        each_peer(lambda step: sq_copy(step).wait_recv())
        sums = proj_sq[...]
        for step in range(1, n):
            sums = sums + proj_sq_in[step]
        inverse = 1.0 / (EPS + jnp.sqrt(sums))
        values = aux_all[...].astype(jnp.float32).reshape(n * groups, 2 * SUB, LANES)
        results = []
        depth = n * real
        for profile in range(2):
            own = values[:, profile * SUB:(profile + 1) * SUB].reshape(n * groups * SUB, LANES)
            if real < groups * SUB:
                starts = range(0, n * groups * SUB, groups * SUB)
                own = jnp.concatenate([own[start:start + real] for start in starts], axis=0)
            norm = jnp.sqrt(jnp.sum(own * own, axis=0, keepdims=True))
            unit_out = (own / (EPS + norm)).astype(jnp.bfloat16)
            unit_in = unit_in_rows(own).astype(jnp.bfloat16)
            skip_out[profile] = lax.dot_general(
                unit_in, unit_out, (((0,), (0,)), ((), ())), preferred_element_type=jnp.float32
            )
            spare = jnp.zeros((proj_w.shape[1] - depth, LANES), jnp.bfloat16)
            tall = jnp.concatenate([unit_out, spare], axis=0)
            weights = (proj_w[...].astype(jnp.float32) * inverse[profile]).astype(jnp.bfloat16)
            results.append(jnp.dot(weights, tall, preferred_element_type=jnp.float32))
        row = lax.broadcasted_iota(jnp.int32, results[0].shape, 0)
        chosen = jnp.where(lax.rem(row, 2 * SUB) < SUB, results[0], results[1])
        m_out[me] = chosen.astype(jnp.bfloat16)
        each_peer(lambda step: m_copy(step).start())

    for copy in fetches(0):
        copy.start()
    for index in range(total):
        if index + 1 < total:
            for copy in fetches(index + 1):
                copy.start()
        for copy in fetches(index):
            copy.wait()
        contract(index)
        if index == 0:
            pl.semaphore_wait(barrier, n + 1)
        near_copy(index).start()
        if index >= 1:
            pass_on(index - 1)
    pass_on(total - 1)

    start_aux()
    offset = 0
    for index in range(1, proj_count + 1):
        start_proj(index, offset)
        offset += cuts[index]
    each_peer(lambda step: sq_copy(step).start())
    finish_map(0)

    def arrived(index):
        each_peer(lambda step: map_spread(index, step).wait_recv())

    def product_of(index, lane, profile):
        half = n // 2
        weights = k_out[index][pl.ds(profile * half, half), :, lane:lane + LANES]
        return jnp.dot(
            tokens[...], weights.reshape(LANES // 2, LANES), preferred_element_type=jnp.float32
        )

    def start_attention():
        each_peer(lambda step: m_copy(step).wait_recv())
        values = m_out[...].astype(jnp.float32).reshape(n * groups, 2 * SUB, LANES)
        for profile in range(2):
            own = values[:, profile * SUB:(profile + 1) * SUB].reshape(n * real, LANES)
            out_rows[profile] = own.astype(jnp.bfloat16)
            skip = jnp.dot(
                tokens[...].astype(jnp.float32), skip_out[profile, 0:LANES // 2],
                preferred_element_type=jnp.float32, precision=lax.Precision.HIGHEST,
            )
            feature[profile] = 0.7 * skip

    def attention(which):
        first, last = plan[which][0]
        heads = list(range(2 * first, 2 * last))
        count = proj.shape[2] // HEAD_DIM
        if which == len(plan) - 1:
            heads.append(count - 1)

        def body(profile, carry):
            found = {}

            def unit(column):
                tile, lane = column // LANES, column % LANES
                if tile not in found:
                    found[tile] = product_of(*places[tile], profile)
                if tile == len(places) - 1:
                    lane = LANES // 2
                own = found[tile][:, lane:lane + HEAD_DIM]
                scale = jnp.sqrt(jnp.mean(own * own, axis=1, keepdims=True))
                return (own * (1.0 / (EPS + scale))).astype(jnp.bfloat16)

            added = jnp.zeros(feature.shape[1:], jnp.float32)
            for head in heads:
                query, keys, values = (
                    unit((part * count + head) * HEAD_DIM) for part in range(3)
                )
                scores = lax.dot_general(
                    query, keys, (((1,), (1,)), ((), ())), preferred_element_type=jnp.float32
                )
                expo = jnp.exp(scores * (1.0 / HEAD_DIM**0.5))
                weights = expo * (1.0 / jnp.sum(expo, axis=1, keepdims=True))
                mixed = jnp.dot(
                    weights.astype(jnp.bfloat16), values, preferred_element_type=jnp.float32
                ).astype(jnp.bfloat16)
                rows_of = out_rows[profile, head * HEAD_DIM:(head + 1) * HEAD_DIM, :]
                added = added + jnp.dot(mixed, rows_of, preferred_element_type=jnp.float32)
            feature[profile] = feature[profile] + 0.3 * added
            return carry

        lax.fori_loop(0, 2, body, 0)

    for index in range(1, maps):
        chunk = index + proj_count
        squares = finish_sum(chunk)
        send_map(index, keep[chunk][0], squares)
        if index == 1:
            out_maps()
            arrived(0)
        elif fused:
            if index == 2:
                start_attention()
            arrived(index - 1)
            attention(index - 2)
        finish_map(index)
    arrived(maps - 1)
    if fused:
        attention(maps - 2)
    else:
        for index in range(1, maps - 1):
            arrived(index)
        each_peer(lambda step: m_copy(step).wait_recv())
        feature[...] = jnp.zeros(feature.shape, feature.dtype)
    for index in range(total):
        near_copy(index).wait_send()
        far_copy(index).wait_send()

    def drain(step):
        for index in range(maps):
            for copy in map_copies(index, step):
                copy.wait_send()
            map_spread(index, step).wait_send()
        aux_copy(step).wait_send()
        sq_copy(step).wait_send()
        m_copy(step).wait_send()

    each_peer(drain)


def exchange_call(coeffs, aux, proj, qkv, tokens, n, real, main_proj, plan, fused):
    snaps, rows, _ = aux.shape
    groups = rows // SUB
    proj_cuts = cut(main_proj, 2)
    cuts = [aux.shape[2]] + proj_cuts
    cuts += [sum(last - first for first, last in parts) * LANES for parts in plan]
    total = len(cuts)
    map_cuts = [LANES] + cuts[1 + len(proj_cuts):]
    maps = len(map_cuts)
    both = 2 * rows
    share = LANES // n
    proj_wide = main_proj + LANES
    kind, wide = jnp.bfloat16, jnp.float32
    shapes = [jax.ShapeDtypeStruct((n, share, width), kind) for width in map_cuts]
    shapes += [
        jax.ShapeDtypeStruct((n, both, LANES), kind),
        jax.ShapeDtypeStruct((2, LANES, LANES), wide),
        jax.ShapeDtypeStruct((2, tokens.shape[0], LANES), wide),
    ]
    scratch = [pltpu.VMEM((2, snaps, rows, max(cuts)), wide)]
    for lead in ((2,), (2,), (2,), (), ()):
        scratch += [pltpu.VMEM(lead + (both, width), kind) for width in cuts]
    scratch += [pltpu.VMEM((n, share, width), kind) for width in map_cuts]
    scratch += [pltpu.VMEM((n, share, width), kind) for width in map_cuts]
    scratch += [pltpu.VMEM((2, 1, width), wide) for width in map_cuts]
    scratch += [pltpu.VMEM((n, 1, width), wide) for width in map_cuts]
    scratch += [
        pltpu.VMEM((n, both, LANES), kind),
        pltpu.VMEM((both, proj_wide), kind),
        pltpu.VMEM((2, 1, proj_wide), wide),
        pltpu.VMEM((n, 2, 1, proj_wide), wide),
        pltpu.VMEM((both, LANES), kind),
        pltpu.VMEM((2, n * real, LANES), kind),
        pltpu.SemaphoreType.DMA((2, 3)),
        pltpu.SemaphoreType.DMA((2, total)),
        pltpu.SemaphoreType.DMA((2, total)),
        pltpu.SemaphoreType.DMA((2, maps, 3, n)),
        pltpu.SemaphoreType.DMA((2, n)),
        pltpu.SemaphoreType.DMA((2, n)),
        pltpu.SemaphoreType.DMA((2, n)),
    ]
    hbm = pl.BlockSpec(memory_space=pl.ANY)
    return pl.pallas_call(
        functools.partial(
            exchange_kernel, plan, tuple(cuts), len(proj_cuts), n, groups, real, fused
        ),
        out_shape=shapes,
        in_specs=[
            pl.BlockSpec(memory_space=pltpu.SMEM), hbm, hbm, hbm,
            pl.BlockSpec(memory_space=pltpu.VMEM),
        ],
        out_specs=[pl.BlockSpec(memory_space=pltpu.VMEM)] * len(shapes),
        scratch_shapes=scratch,
        compiler_params=pltpu.CompilerParams(
            collective_id=0, has_side_effects=True, vmem_limit_bytes=60 * 2**20
        ),
    )(coeffs, aux, proj, qkv, tokens)


def shards(snap_in, snap_qkv, snap_proj, snap_out, coeffs, latent, levels):
    owned = PROF // lax.axis_size("snap")
    n = lax.axis_size("param")
    width = snap_proj.shape[2]
    rows = snap_qkv.shape[1]
    main_proj = width // LANES * LANES
    main_qkv = snap_qkv.shape[2] // LANES * LANES
    aux = jnp.concatenate(
        [snap_in.transpose(0, 2, 1), snap_out, snap_proj[:, :, main_proj:], snap_qkv[:, :, main_qkv:]],
        axis=2,
    )
    main = [snap_proj, snap_qkv]
    spare = -rows % SUB
    if spare:
        aux, *main = [jnp.pad(x, ((0, 0), (0, spare), (0, 0))) for x in [aux] + main]
    plan = head_plan(width // LANES)
    share = owned * snap_in.shape[1] // n
    fused = rows % SUB == 0 and share % (2 * SUB) == 0 and latent.shape[0] == 1
    tokens, c_skip, c_out = prepare(latent, levels)
    *maps, out_map, skip_map, feature = exchange_call(
        coeffs, aux, main[0], main[1], tokens, n, rows, main_proj, plan, fused
    )
    half = LANES // 2
    if fused:
        feature = feature[:, :, half:] / jnp.sqrt(0.58)
        return jax.vmap(lambda value: finish(value, latent, c_skip, c_out))(feature)
    maps = [part.reshape(owned, -1, part.shape[2]) for part in maps]
    places = tile_places(plan)
    tiles = []
    for tile in range(len(places) - 1):
        index, lane = places[tile]
        tiles.append(maps[index][:, :, lane:lane + LANES])
    qkv_map = jnp.concatenate(tiles + [maps[0][:, :, half:]], axis=2)
    out_map = out_map.reshape(n, -1, owned, SUB, LANES)[..., half:]
    out_map = out_map.transpose(2, 0, 1, 3, 4).reshape(owned, n, -1, half)[:, :, :rows]
    out_map = out_map.reshape(owned, n * rows, half)
    skip_map = skip_map[:, :half, half:]
    results = []
    for profile in range(owned):
        feature = attend(tokens, qkv_map[profile], out_map[profile], skip_map[profile])
        results.append(finish(feature, latent, c_skip, c_out))
    return jnp.stack(results)


def solution(mesh):
    in_specs = (
        P("snap", None, "param"),
        P("snap", "param", None),
        P("snap", "param", None),
        P("snap", "param", None),
        P("snap", None),
        P("param", None, None),
        P("param"),
    )
    out_specs = P("snap", "param", None, None)
    return jax.shard_map(shards, mesh=mesh, in_specs=in_specs, out_specs=out_specs, check_vma=False)
```

```python
import functools

import jax
import jax.numpy as jnp
from jax import lax
from jax.experimental import pallas as pl
from jax.experimental.pallas import tpu as pltpu
from jax.sharding import PartitionSpec as P

HEAD_DIM = 64
PROF = 8
NLEV = 16


EPS = 0.0001


def noise_scales(levels):
    step = levels.astype(jnp.float32) / (NLEV - 1)
    sigma = jnp.exp(jnp.log(0.2) + step * (jnp.log(5.0) - jnp.log(0.2)))
    square = sigma * sigma + 0.25
    return (1.0 / jnp.sqrt(square), 0.25 / square, 0.5 * sigma / jnp.sqrt(square))


def to_tokens(image):
    count = image.shape[0]
    parts = image.reshape(count, 16, 4, 16, 4, 4).transpose(0, 1, 3, 2, 4, 5)
    return parts.reshape(count, 256, 64)


def from_tokens(feature):
    count = feature.shape[0]
    parts = feature.reshape(count, 16, 16, 4, 4, 4).transpose(0, 1, 3, 2, 4, 5)
    return parts.reshape(count, 64, 256)


def head_unit(values):
    scale = jnp.sqrt(jnp.mean(values * values, axis=-1, keepdims=True))
    return (values / (EPS + scale)).astype(jnp.bfloat16)


def inverse_norms(sums):
    return 1.0 / (EPS + jnp.sqrt(sums))


def attend(tokens, mixed_qkv, mixed_out, skip_map):
    rows = tokens.shape[0]
    count = rows // 256
    width = mixed_out.shape[0]
    heads = width // HEAD_DIM
    qkv = jnp.dot(tokens, mixed_qkv, preferred_element_type=jnp.float32)
    qkv = head_unit(qkv.reshape(count, 256, 3, heads, HEAD_DIM))
    query = qkv[:, :, 0]
    keys = qkv[:, :, 1]
    values = qkv[:, :, 2]
    scores = jnp.einsum("bqhd,bkhd->bhqk", query, keys, preferred_element_type=jnp.float32)
    scores = scores * (1.0 / jnp.sqrt(float(HEAD_DIM)))
    expo = jnp.exp(scores)
    weights = (expo / jnp.sum(expo, axis=-1, keepdims=True)).astype(jnp.bfloat16)
    attended = jnp.einsum("bhqk,bkhd->bqhd", weights, values, preferred_element_type=jnp.float32)
    attended = attended.astype(jnp.bfloat16).reshape(rows, width)
    skip = jnp.dot(tokens.astype(jnp.float32), skip_map, precision=lax.Precision.HIGHEST)
    mapped = jnp.dot(attended, mixed_out, preferred_element_type=jnp.float32)
    return (0.7 * skip + 0.3 * mapped) / jnp.sqrt(0.58)


def prepare(latent, levels):
    c_in, c_skip, c_out = noise_scales(levels)
    count = latent.shape[0]
    tokens = to_tokens(c_in[:, None, None] * latent).reshape(count * 256, 64).astype(jnp.bfloat16)
    return (tokens, c_skip, c_out)


def finish(feature, latent, c_skip, c_out):
    count = latent.shape[0]
    image = from_tokens(feature.reshape(count, 256, 64))
    return c_skip[:, None, None] * latent + c_out[:, None, None] * image


LANES = 128
SUB = 8
PIECE = 512


def cut(width, pieces):
    tiles = width // LANES
    sizes = [tiles // pieces + (1 if i < tiles % pieces else 0) for i in range(pieces)]
    return [size * LANES for size in sizes if size]


def head_plan(pairs):
    sizes = cut(pairs * LANES, 5)
    sizes = [size // LANES for size in sizes]
    if len(sizes) > 2 and sizes[-1] > 1:
        sizes[0] += 1
        sizes[-1] -= 1
    plan = []
    first = 0
    for size in sizes:
        last = first + size
        key_first = first + 1 if first else 0
        plan.append(
            (
                (first, last),
                (pairs + key_first, pairs + last + 1),
                (2 * pairs + 1 + first, 2 * pairs + 1 + last),
            )
        )
        first = last
    return tuple(plan)


def tile_places(plan):
    places = {}
    for index, parts in enumerate(plan):
        lane = 0
        for first, last in parts:
            for tile in range(first, last):
                places[tile] = (index + 1, lane)
                lane += LANES
    places[len(places)] = (0, 0)
    return places


def exchange_kernel(
    plan, cuts, proj_count, n, groups, real, fused,
    coeffs, aux, proj, qkv, tokens,
    *refs,
):
    total = len(cuts)
    maps = total - proj_count
    places = tile_places(plan)
    pos = 0

    def take(count):
        nonlocal pos
        pos += count
        return refs[pos - count:pos]

    k_out = take(maps)
    (m_out, skip_out, feature) = take(3)
    (feed,) = take(1)
    away, keep, near, over, far = (take(total) for _ in range(5))
    g_send, g_recv, q_send, q_recv = (take(maps) for _ in range(4))
    (aux_all, proj_w, proj_sq, proj_sq_in, unit_rows, out_rows, spread) = take(7)
    (feed_sem, near_sems, far_sems, map_sems, aux_sems, sq_sems, m_sems) = take(7)

    rows = groups * 2 * SUB
    snap = lax.axis_index("snap")
    me = lax.axis_index("param")
    core = lax.rem(snap, 2)
    sibling = snap + 1 - 2 * core
    across = lax.rem(snap + 2, 4)

    def peer(step):
        return {"snap": snap, "param": lax.rem(me + step, n)}

    barrier = pltpu.get_barrier_semaphore()
    for other in (sibling, across):
        pl.semaphore_signal(
            barrier, inc=1, device_id={"snap": other, "param": me},
            device_id_type=pl.DeviceIdType.MESH,
        )

    def greet(step, carry):
        pl.semaphore_signal(
            barrier, inc=1, device_id=peer(step), device_id_type=pl.DeviceIdType.MESH
        )
        return carry

    lax.fori_loop(1, n, greet, 0)

    starts = [[(0, cuts[0])]]
    for index in range(proj_count):
        starts.append([(sum(cuts[1:1 + index]), cuts[1 + index])])
    for parts in plan:
        starts.append([(first * LANES, (last - first) * LANES) for first, last in parts])
    sources = [aux] + [proj] * proj_count + [qkv] * len(plan)

    def fetches(index):
        slot = index % 2
        copies = []
        at = 0
        for which, (start, width) in enumerate(starts[index]):
            copies.append(
                pltpu.make_async_copy(
                    sources[index].at[:, :, start:start + width],
                    feed.at[slot, :, :, at:at + width],
                    feed_sem.at[slot, which],
                )
            )
            at += width
        return copies

    def remote(source, target, sems, at, device):
        return pltpu.make_async_remote_copy(
            src_ref=source, dst_ref=target, send_sem=sems.at[(0,) + at], recv_sem=sems.at[(1,) + at],
            device_id=device, device_id_type=pl.DeviceIdType.MESH,
        )

    def near_copy(index):
        return remote(away[index], near[index], near_sems, (index,), {"snap": sibling, "param": me})

    def far_copy(index):
        return remote(over[index], far[index], far_sems, (index,), {"snap": across, "param": me})

    def each_peer(act):
        def body(step, carry):
            act(step)
            return carry

        lax.fori_loop(1, n, body, 0)

    def map_copies(index, step):
        goal = lax.rem(me + step, n)
        half = (goal * 2) // n
        return (
            remote(g_send[index].at[goal], g_recv[index].at[step], map_sems, (index, 0, step), peer(step)),
            remote(q_send[index].at[half], q_recv[index].at[step], map_sems, (index, 1, step), peer(step)),
        )

    def map_spread(index, step):
        return remote(
            k_out[index].at[me], k_out[index].at[me], map_sems, (index, 2, step), peer(step)
        )

    def aux_copy(step):
        return remote(aux_all.at[me], aux_all.at[me], aux_sems, (step,), peer(step))

    def sq_copy(step):
        return remote(proj_sq, proj_sq_in.at[step], sq_sems, (step,), peer(step))

    def m_copy(step):
        return remote(m_out.at[me], m_out.at[me], m_sems, (step,), peer(step))

    pairs = (snap, across, sibling, lax.rem(sibling + 2, 4))

    count = feed.shape[1]
    for pair in range(4):
        for which in range(2):
            for s in range(count):
                spread[2 * pair + which, s] = jnp.full(
                    (SUB, LANES), coeffs[s, 2 * pairs[pair] + which], jnp.float32
                )

    def contract(index):
        width = cuts[index]
        slot = index % 2

        def body(group, carry):
            at = pl.ds(pl.multiple_of(group * SUB, SUB), SUB)
            to = pl.ds(pl.multiple_of(group * 2 * SUB, 2 * SUB), 2 * SUB)
            for start in range(0, width, PIECE):
                pieces = [
                    slice(lane, lane + LANES)
                    for lane in range(start, min(start + PIECE, width), LANES)
                ]
                snaps = [[feed[slot, s, at, piece] for piece in pieces] for s in range(count)]
                for pair in range(4):
                    both = []
                    for column in (2 * pair, 2 * pair + 1):
                        factor = spread[column, 0]
                        values = [factor * snap_piece for snap_piece in snaps[0]]
                        for s in range(1, count):
                            factor = spread[column, s]
                            values = [
                                value + factor * snap_piece
                                for value, snap_piece in zip(values, snaps[s])
                            ]
                        both.append(values)
                    for piece, first, second in zip(pieces, *both):
                        packed = jnp.concatenate([first, second], axis=0).astype(jnp.bfloat16)
                        if pair < 2:
                            keep[index][pair, to, piece] = packed
                        else:
                            away[index][pair - 2, to, piece] = packed
            return carry

        lax.fori_loop(0, groups, body, 0)

    def pass_on(index):
        near_copy(index).wait_recv()

        def body(group, carry):
            to = pl.ds(pl.multiple_of(group * 2 * SUB, 2 * SUB), 2 * SUB)
            own = keep[index][1, to, :].astype(jnp.float32) + near[index][1, to, :].astype(jnp.float32)
            over[index][to, :] = own.astype(jnp.bfloat16)
            return carry

        lax.fori_loop(0, groups, body, 0)
        far_copy(index).start()

    def finish_sum(index):
        far_copy(index).wait_recv()

        def body(group, squares):
            to = pl.ds(pl.multiple_of(group * 2 * SUB, 2 * SUB), 2 * SUB)
            own = keep[index][0, to, :].astype(jnp.float32) + near[index][0, to, :].astype(jnp.float32)
            own = own + far[index][to, :].astype(jnp.float32)
            keep[index][0, to, :] = own.astype(jnp.bfloat16)
            return squares + own * own

        start = jnp.zeros((2 * SUB, cuts[index]), jnp.float32)
        squares = lax.fori_loop(0, groups, body, start)
        return (
            jnp.sum(squares[:SUB], axis=0, keepdims=True),
            jnp.sum(squares[SUB:], axis=0, keepdims=True),
        )

    def send_map(index, weights, squares):
        product = lax.dot_general(
            unit_rows[...], weights, (((0,), (0,)), ((), ())), preferred_element_type=jnp.float32
        ).astype(jnp.bfloat16)
        share = g_send[index].shape[1]
        for goal in range(n):
            g_send[index][goal] = product[goal * share:(goal + 1) * share]
        q_send[index][0] = squares[0]
        q_send[index][1] = squares[1]

        def act(step):
            for copy in map_copies(index, step):
                copy.start()

        each_peer(act)

    def finish_map(index):
        def act(step):
            for copy in map_copies(index, step):
                copy.wait_recv()

        each_peer(act)
        product = g_send[index][me].astype(jnp.float32)
        squares = q_send[index][(me * 2) // n]
        for step in range(1, n):
            product = product + g_recv[index][step].astype(jnp.float32)
            squares = squares + q_recv[index][step]
        scaled = product * (1.0 / (EPS + jnp.sqrt(squares)))
        k_out[index][me] = scaled.astype(jnp.bfloat16)
        each_peer(lambda step: map_spread(index, step).start())

    def unit_in_rows(values):
        lane = lax.broadcasted_iota(jnp.int32, values.shape, 1)
        left = jnp.where(lane < LANES // 2, values, 0.0)
        norm = jnp.sqrt(jnp.sum(left * left, axis=1, keepdims=True))
        return left / (EPS + norm)

    def start_aux():
        squares = finish_sum(0)
        own = keep[0][0, :, 0:LANES]
        aux_all[me] = own
        each_peer(lambda step: aux_copy(step).start())
        unit = unit_in_rows(own.astype(jnp.float32))
        unit = unit + pltpu.roll(unit, LANES // 2, 1)
        row = lax.broadcasted_iota(jnp.int32, unit.shape, 0)
        lane = lax.broadcasted_iota(jnp.int32, unit.shape, 1)
        same = lax.rem(row, 2 * SUB) // SUB == lane // (LANES // 2)
        unit_rows[...] = jnp.where(same, unit, 0.0).astype(jnp.bfloat16)
        rest = keep[0][0, :, LANES:]
        proj_width = proj_w.shape[1] - LANES
        proj_w[:, proj_width:] = jnp.where(lane < LANES // 2, rest, jnp.zeros_like(rest))
        first = lax.broadcasted_iota(jnp.int32, (1, LANES), 1) < LANES // 2
        for profile in range(2):
            proj_sq[profile, :, proj_width:] = jnp.where(first, squares[profile][:, LANES:], 0.0)
        send_map(0, rest, [square[:, LANES:] for square in squares])

    def start_proj(index, offset):
        squares = finish_sum(index)
        proj_w[:, offset:offset + cuts[index]] = keep[index][0]
        for profile in range(2):
            proj_sq[profile, :, offset:offset + cuts[index]] = squares[profile]

    def out_maps():
        each_peer(lambda step: aux_copy(step).wait_recv())
        each_peer(lambda step: sq_copy(step).wait_recv())
        sums = proj_sq[...]
        for step in range(1, n):
            sums = sums + proj_sq_in[step]
        inverse = 1.0 / (EPS + jnp.sqrt(sums))
        values = aux_all[...].astype(jnp.float32).reshape(n * groups, 2 * SUB, LANES)
        results = []
        depth = n * real
        for profile in range(2):
            own = values[:, profile * SUB:(profile + 1) * SUB].reshape(n * groups * SUB, LANES)
            if real < groups * SUB:
                starts = range(0, n * groups * SUB, groups * SUB)
                own = jnp.concatenate([own[start:start + real] for start in starts], axis=0)
            norm = jnp.sqrt(jnp.sum(own * own, axis=0, keepdims=True))
            unit_out = (own / (EPS + norm)).astype(jnp.bfloat16)
            unit_in = unit_in_rows(own).astype(jnp.bfloat16)
            skip_out[profile] = lax.dot_general(
                unit_in, unit_out, (((0,), (0,)), ((), ())), preferred_element_type=jnp.float32
            )
            spare = jnp.zeros((proj_w.shape[1] - depth, LANES), jnp.bfloat16)
            tall = jnp.concatenate([unit_out, spare], axis=0)
            weights = (proj_w[...].astype(jnp.float32) * inverse[profile]).astype(jnp.bfloat16)
            results.append(jnp.dot(weights, tall, preferred_element_type=jnp.float32))
        row = lax.broadcasted_iota(jnp.int32, results[0].shape, 0)
        chosen = jnp.where(lax.rem(row, 2 * SUB) < SUB, results[0], results[1])
        m_out[me] = chosen.astype(jnp.bfloat16)
        each_peer(lambda step: m_copy(step).start())

    for copy in fetches(0):
        copy.start()
    for index in range(total):
        if index + 1 < total:
            for copy in fetches(index + 1):
                copy.start()
        for copy in fetches(index):
            copy.wait()
        contract(index)
        if index == 0:
            pl.semaphore_wait(barrier, n + 1)
        near_copy(index).start()
        if index >= 1:
            pass_on(index - 1)
    pass_on(total - 1)

    start_aux()
    offset = 0
    for index in range(1, proj_count + 1):
        start_proj(index, offset)
        offset += cuts[index]
    each_peer(lambda step: sq_copy(step).start())
    finish_map(0)

    def arrived(index):
        each_peer(lambda step: map_spread(index, step).wait_recv())

    def product_of(index, lane, profile):
        half = n // 2
        weights = k_out[index][pl.ds(profile * half, half), :, lane:lane + LANES]
        return jnp.dot(
            tokens[...], weights.reshape(LANES // 2, LANES), preferred_element_type=jnp.float32
        )

    def start_attention():
        each_peer(lambda step: m_copy(step).wait_recv())
        values = m_out[...].astype(jnp.float32).reshape(n * groups, 2 * SUB, LANES)
        for profile in range(2):
            own = values[:, profile * SUB:(profile + 1) * SUB].reshape(n * real, LANES)
            out_rows[profile] = own.astype(jnp.bfloat16)
            skip = jnp.dot(
                tokens[...].astype(jnp.float32), skip_out[profile, 0:LANES // 2],
                preferred_element_type=jnp.float32, precision=lax.Precision.HIGHEST,
            )
            feature[profile] = 0.7 * skip

    def attention(which):
        first, last = plan[which][0]
        heads = list(range(2 * first, 2 * last))
        count = proj.shape[2] // HEAD_DIM
        if which == len(plan) - 1:
            heads.append(count - 1)

        def body(profile, carry):
            found = {}

            def unit(column):
                tile, lane = column // LANES, column % LANES
                if tile not in found:
                    found[tile] = product_of(*places[tile], profile)
                if tile == len(places) - 1:
                    lane = LANES // 2
                own = found[tile][:, lane:lane + HEAD_DIM]
                scale = jnp.sqrt(jnp.mean(own * own, axis=1, keepdims=True))
                return (own * (1.0 / (EPS + scale))).astype(jnp.bfloat16)

            added = jnp.zeros(feature.shape[1:], jnp.float32)
            for head in heads:
                query, keys, values = (
                    unit((part * count + head) * HEAD_DIM) for part in range(3)
                )
                scores = lax.dot_general(
                    query, keys, (((1,), (1,)), ((), ())), preferred_element_type=jnp.float32
                )
                expo = jnp.exp(scores * (1.0 / HEAD_DIM**0.5))
                weights = expo * (1.0 / jnp.sum(expo, axis=1, keepdims=True))
                mixed = jnp.dot(
                    weights.astype(jnp.bfloat16), values, preferred_element_type=jnp.float32
                ).astype(jnp.bfloat16)
                rows_of = out_rows[profile, head * HEAD_DIM:(head + 1) * HEAD_DIM, :]
                added = added + jnp.dot(mixed, rows_of, preferred_element_type=jnp.float32)
            feature[profile] = feature[profile] + 0.3 * added
            return carry

        lax.fori_loop(0, 2, body, 0)

    for index in range(1, maps):
        chunk = index + proj_count
        squares = finish_sum(chunk)
        send_map(index, keep[chunk][0], squares)
        if index == 1:
            out_maps()
            arrived(0)
        elif fused:
            if index == 2:
                start_attention()
            arrived(index - 1)
            attention(index - 2)
        finish_map(index)
    arrived(maps - 1)
    if fused:
        attention(maps - 2)
    else:
        for index in range(1, maps - 1):
            arrived(index)
        each_peer(lambda step: m_copy(step).wait_recv())
        feature[...] = jnp.zeros(feature.shape, feature.dtype)
    for index in range(total):
        near_copy(index).wait_send()
        far_copy(index).wait_send()

    def drain(step):
        for index in range(maps):
            for copy in map_copies(index, step):
                copy.wait_send()
            map_spread(index, step).wait_send()
        aux_copy(step).wait_send()
        sq_copy(step).wait_send()
        m_copy(step).wait_send()

    each_peer(drain)


def exchange_call(coeffs, aux, proj, qkv, tokens, n, real, main_proj, plan, fused):
    snaps, rows, _ = aux.shape
    groups = rows // SUB
    proj_cuts = cut(main_proj, 2)
    cuts = [aux.shape[2]] + proj_cuts
    cuts += [sum(last - first for first, last in parts) * LANES for parts in plan]
    total = len(cuts)
    map_cuts = [LANES] + cuts[1 + len(proj_cuts):]
    maps = len(map_cuts)
    both = 2 * rows
    share = LANES // n
    proj_wide = main_proj + LANES
    kind, wide = jnp.bfloat16, jnp.float32
    shapes = [jax.ShapeDtypeStruct((n, share, width), kind) for width in map_cuts]
    shapes += [
        jax.ShapeDtypeStruct((n, both, LANES), kind),
        jax.ShapeDtypeStruct((2, LANES, LANES), wide),
        jax.ShapeDtypeStruct((2, tokens.shape[0], LANES), wide),
    ]
    scratch = [pltpu.VMEM((2, snaps, rows, max(cuts)), wide)]
    for lead in ((2,), (2,), (2,), (), ()):
        scratch += [pltpu.VMEM(lead + (both, width), kind) for width in cuts]
    scratch += [pltpu.VMEM((n, share, width), kind) for width in map_cuts]
    scratch += [pltpu.VMEM((n, share, width), kind) for width in map_cuts]
    scratch += [pltpu.VMEM((2, 1, width), wide) for width in map_cuts]
    scratch += [pltpu.VMEM((n, 1, width), wide) for width in map_cuts]
    scratch += [
        pltpu.VMEM((n, both, LANES), kind),
        pltpu.VMEM((both, proj_wide), kind),
        pltpu.VMEM((2, 1, proj_wide), wide),
        pltpu.VMEM((n, 2, 1, proj_wide), wide),
        pltpu.VMEM((both, LANES), kind),
        pltpu.VMEM((2, n * real, LANES), kind),
        pltpu.VMEM((coeffs.shape[1], snaps, SUB, LANES), wide),
        pltpu.SemaphoreType.DMA((2, 3)),
        pltpu.SemaphoreType.DMA((2, total)),
        pltpu.SemaphoreType.DMA((2, total)),
        pltpu.SemaphoreType.DMA((2, maps, 3, n)),
        pltpu.SemaphoreType.DMA((2, n)),
        pltpu.SemaphoreType.DMA((2, n)),
        pltpu.SemaphoreType.DMA((2, n)),
    ]
    hbm = pl.BlockSpec(memory_space=pl.ANY)
    return pl.pallas_call(
        functools.partial(
            exchange_kernel, plan, tuple(cuts), len(proj_cuts), n, groups, real, fused
        ),
        out_shape=shapes,
        in_specs=[
            pl.BlockSpec(memory_space=pltpu.SMEM), hbm, hbm, hbm,
            pl.BlockSpec(memory_space=pltpu.VMEM),
        ],
        out_specs=[pl.BlockSpec(memory_space=pltpu.VMEM)] * len(shapes),
        scratch_shapes=scratch,
        compiler_params=pltpu.CompilerParams(
            collective_id=0, has_side_effects=True, vmem_limit_bytes=60 * 2**20
        ),
    )(coeffs, aux, proj, qkv, tokens)


def shards(snap_in, snap_qkv, snap_proj, snap_out, coeffs, latent, levels):
    owned = PROF // lax.axis_size("snap")
    n = lax.axis_size("param")
    width = snap_proj.shape[2]
    rows = snap_qkv.shape[1]
    main_proj = width // LANES * LANES
    main_qkv = snap_qkv.shape[2] // LANES * LANES
    aux = jnp.concatenate(
        [snap_in.transpose(0, 2, 1), snap_out, snap_proj[:, :, main_proj:], snap_qkv[:, :, main_qkv:]],
        axis=2,
    )
    main = [snap_proj, snap_qkv]
    spare = -rows % SUB
    if spare:
        aux, *main = [jnp.pad(x, ((0, 0), (0, spare), (0, 0))) for x in [aux] + main]
    plan = head_plan(width // LANES)
    share = owned * snap_in.shape[1] // n
    fused = rows % SUB == 0 and share % (2 * SUB) == 0 and latent.shape[0] == 1
    tokens, c_skip, c_out = prepare(latent, levels)
    *maps, out_map, skip_map, feature = exchange_call(
        coeffs, aux, main[0], main[1], tokens, n, rows, main_proj, plan, fused
    )
    half = LANES // 2
    if fused:
        feature = feature[:, :, half:] / jnp.sqrt(0.58)
        return jnp.stack([finish(feature[p], latent, c_skip, c_out) for p in range(owned)])
    maps = [part.reshape(owned, -1, part.shape[2]) for part in maps]
    places = tile_places(plan)
    tiles = []
    for tile in range(len(places) - 1):
        index, lane = places[tile]
        tiles.append(maps[index][:, :, lane:lane + LANES])
    qkv_map = jnp.concatenate(tiles + [maps[0][:, :, half:]], axis=2)
    out_map = out_map.reshape(n, -1, owned, SUB, LANES)[..., half:]
    out_map = out_map.transpose(2, 0, 1, 3, 4).reshape(owned, n, -1, half)[:, :, :rows]
    out_map = out_map.reshape(owned, n * rows, half)
    skip_map = skip_map[:, :half, half:]
    results = []
    for profile in range(owned):
        feature = attend(tokens, qkv_map[profile], out_map[profile], skip_map[profile])
        results.append(finish(feature, latent, c_skip, c_out))
    return jnp.stack(results)


def solution(mesh):
    in_specs = (
        P("snap", None, "param"),
        P("snap", "param", None),
        P("snap", "param", None),
        P("snap", "param", None),
        P("snap", None),
        P("param", None, None),
        P("param"),
    )
    out_specs = P("snap", "param", None, None)
    return jax.shard_map(shards, mesh=mesh, in_specs=in_specs, out_specs=out_specs, check_vma=False)
```

```python
import functools

import jax
import jax.numpy as jnp
from jax import lax
from jax.experimental import pallas as pl
from jax.experimental.pallas import tpu as pltpu
from jax.sharding import PartitionSpec as P

HEAD_DIM = 64
PROF = 8
NLEV = 16


EPS = 0.0001


def noise_scales(levels):
    step = levels.astype(jnp.float32) / (NLEV - 1)
    sigma = jnp.exp(jnp.log(0.2) + step * (jnp.log(5.0) - jnp.log(0.2)))
    square = sigma * sigma + 0.25
    return (1.0 / jnp.sqrt(square), 0.25 / square, 0.5 * sigma / jnp.sqrt(square))


def to_tokens(image):
    count = image.shape[0]
    parts = image.reshape(count, 16, 4, 16, 4, 4).transpose(0, 1, 3, 2, 4, 5)
    return parts.reshape(count, 256, 64)


def from_tokens(feature):
    count = feature.shape[0]
    parts = feature.reshape(count, 16, 16, 4, 4, 4).transpose(0, 1, 3, 2, 4, 5)
    return parts.reshape(count, 64, 256)


def head_unit(values):
    scale = jnp.sqrt(jnp.mean(values * values, axis=-1, keepdims=True))
    return (values / (EPS + scale)).astype(jnp.bfloat16)


def inverse_norms(sums):
    return 1.0 / (EPS + jnp.sqrt(sums))


def attend(tokens, mixed_qkv, mixed_out, skip_map):
    rows = tokens.shape[0]
    count = rows // 256
    width = mixed_out.shape[0]
    heads = width // HEAD_DIM
    qkv = jnp.dot(tokens, mixed_qkv, preferred_element_type=jnp.float32)
    qkv = head_unit(qkv.reshape(count, 256, 3, heads, HEAD_DIM))
    query = qkv[:, :, 0]
    keys = qkv[:, :, 1]
    values = qkv[:, :, 2]
    scores = jnp.einsum("bqhd,bkhd->bhqk", query, keys, preferred_element_type=jnp.float32)
    scores = scores * (1.0 / jnp.sqrt(float(HEAD_DIM)))
    expo = jnp.exp(scores)
    weights = (expo / jnp.sum(expo, axis=-1, keepdims=True)).astype(jnp.bfloat16)
    attended = jnp.einsum("bhqk,bkhd->bqhd", weights, values, preferred_element_type=jnp.float32)
    attended = attended.astype(jnp.bfloat16).reshape(rows, width)
    skip = jnp.dot(tokens.astype(jnp.float32), skip_map, precision=lax.Precision.HIGHEST)
    mapped = jnp.dot(attended, mixed_out, preferred_element_type=jnp.float32)
    return (0.7 * skip + 0.3 * mapped) / jnp.sqrt(0.58)


def prepare(latent, levels):
    c_in, c_skip, c_out = noise_scales(levels)
    count = latent.shape[0]
    tokens = to_tokens(c_in[:, None, None] * latent).reshape(count * 256, 64).astype(jnp.bfloat16)
    return (tokens, c_skip, c_out)


def finish(feature, latent, c_skip, c_out):
    count = latent.shape[0]
    image = from_tokens(feature.reshape(count, 256, 64))
    return c_skip[:, None, None] * latent + c_out[:, None, None] * image


LANES = 128
SUB = 8
PIECE = 512


def cut(width, pieces):
    tiles = width // LANES
    sizes = [tiles // pieces + (1 if i < tiles % pieces else 0) for i in range(pieces)]
    return [size * LANES for size in sizes if size]


def head_plan(pairs):
    sizes = cut(pairs * LANES, 5)
    sizes = [size // LANES for size in sizes]
    if len(sizes) > 2 and sizes[-1] > 1:
        sizes[0] += 1
        sizes[-1] -= 1
    plan = []
    first = 0
    for size in sizes:
        last = first + size
        key_first = first + 1 if first else 0
        plan.append(
            (
                (first, last),
                (pairs + key_first, pairs + last + 1),
                (2 * pairs + 1 + first, 2 * pairs + 1 + last),
            )
        )
        first = last
    return tuple(plan)


def tile_places(plan):
    places = {}
    for index, parts in enumerate(plan):
        lane = 0
        for first, last in parts:
            for tile in range(first, last):
                places[tile] = (index + 1, lane)
                lane += LANES
    places[len(places)] = (0, 0)
    return places


def exchange_kernel(
    plan, cuts, proj_count, n, groups, real, fused,
    coeffs, aux, proj, qkv, tokens,
    *refs,
):
    total = len(cuts)
    maps = total - proj_count
    places = tile_places(plan)
    pos = 0

    def take(count):
        nonlocal pos
        pos += count
        return refs[pos - count:pos]

    k_out = take(maps)
    (m_out, skip_out, feature) = take(3)
    (feed,) = take(1)
    away, keep, near, over, far = (take(total) for _ in range(5))
    g_send, g_recv, q_send, q_recv = (take(maps) for _ in range(4))
    (aux_all, proj_w, proj_sq, proj_sq_in, unit_rows, out_rows, spread) = take(7)
    (feed_sem, near_sems, far_sems, map_sems, aux_sems, sq_sems, m_sems) = take(7)

    rows = groups * 2 * SUB
    snap = lax.axis_index("snap")
    me = lax.axis_index("param")
    core = lax.rem(snap, 2)
    sibling = snap + 1 - 2 * core
    across = lax.rem(snap + 2, 4)

    def peer(step):
        return {"snap": snap, "param": lax.rem(me + step, n)}

    barrier = pltpu.get_barrier_semaphore()
    for other in (sibling, across):
        pl.semaphore_signal(
            barrier, inc=1, device_id={"snap": other, "param": me},
            device_id_type=pl.DeviceIdType.MESH,
        )

    def greet(step, carry):
        pl.semaphore_signal(
            barrier, inc=1, device_id=peer(step), device_id_type=pl.DeviceIdType.MESH
        )
        return carry

    lax.fori_loop(1, n, greet, 0)

    starts = [[(0, cuts[0])]]
    for index in range(proj_count):
        starts.append([(sum(cuts[1:1 + index]), cuts[1 + index])])
    for parts in plan:
        starts.append([(first * LANES, (last - first) * LANES) for first, last in parts])
    sources = [aux] + [proj] * proj_count + [qkv] * len(plan)

    def fetches(index):
        slot = index % 2
        copies = []
        at = 0
        for which, (start, width) in enumerate(starts[index]):
            copies.append(
                pltpu.make_async_copy(
                    sources[index].at[:, :, start:start + width],
                    feed.at[slot, :, :, at:at + width],
                    feed_sem.at[slot, which],
                )
            )
            at += width
        return copies

    def remote(source, target, sems, at, device):
        return pltpu.make_async_remote_copy(
            src_ref=source, dst_ref=target, send_sem=sems.at[(0,) + at], recv_sem=sems.at[(1,) + at],
            device_id=device, device_id_type=pl.DeviceIdType.MESH,
        )

    def near_copy(index):
        return remote(away[index], near[index], near_sems, (index,), {"snap": sibling, "param": me})

    def far_copy(index):
        return remote(over[index], far[index], far_sems, (index,), {"snap": across, "param": me})

    def each_peer(act):
        def body(step, carry):
            act(step)
            return carry

        lax.fori_loop(1, n, body, 0)

    def map_copies(index, step):
        goal = lax.rem(me + step, n)
        half = (goal * 2) // n
        return (
            remote(g_send[index].at[goal], g_recv[index].at[step], map_sems, (index, 0, step), peer(step)),
            remote(q_send[index].at[half], q_recv[index].at[step], map_sems, (index, 1, step), peer(step)),
        )

    def map_spread(index, step):
        return remote(
            k_out[index].at[me], k_out[index].at[me], map_sems, (index, 2, step), peer(step)
        )

    def aux_copy(step):
        return remote(aux_all.at[me], aux_all.at[me], aux_sems, (step,), peer(step))

    def sq_copy(step):
        return remote(proj_sq, proj_sq_in.at[step], sq_sems, (step,), peer(step))

    def m_copy(step):
        return remote(m_out.at[me], m_out.at[me], m_sems, (step,), peer(step))

    pairs = (snap, across, sibling, lax.rem(sibling + 2, 4))

    count = feed.shape[1]
    for pair in range(4):
        for which in range(2):
            for s in range(count):
                spread[2 * pair + which, s] = jnp.full(
                    (SUB, LANES), coeffs[s, 2 * pairs[pair] + which], jnp.float32
                )

    def contract(index):
        width = cuts[index]
        slot = index % 2

        def body(group, carry):
            at = pl.ds(pl.multiple_of(group * SUB, SUB), SUB)
            to = pl.ds(pl.multiple_of(group * 2 * SUB, 2 * SUB), 2 * SUB)
            for start in range(0, width, PIECE):
                pieces = [
                    slice(lane, lane + LANES)
                    for lane in range(start, min(start + PIECE, width), LANES)
                ]
                snaps = [[feed[slot, s, at, piece] for piece in pieces] for s in range(count)]
                for pair in range(4):
                    both = []
                    for column in (2 * pair, 2 * pair + 1):
                        factor = spread[column, 0]
                        values = [factor * snap_piece for snap_piece in snaps[0]]
                        for s in range(1, count):
                            factor = spread[column, s]
                            values = [
                                value + factor * snap_piece
                                for value, snap_piece in zip(values, snaps[s])
                            ]
                        both.append(values)
                    for piece, first, second in zip(pieces, *both):
                        packed = jnp.concatenate([first, second], axis=0).astype(jnp.bfloat16)
                        if pair < 2:
                            keep[index][pair, to, piece] = packed
                        else:
                            away[index][pair - 2, to, piece] = packed
            return carry

        lax.fori_loop(0, groups, body, 0)

    def pass_on(index):
        near_copy(index).wait_recv()

        def body(group, carry):
            to = pl.ds(pl.multiple_of(group * 2 * SUB, 2 * SUB), 2 * SUB)
            own = keep[index][1, to, :].astype(jnp.float32) + near[index][1, to, :].astype(jnp.float32)
            over[index][to, :] = own.astype(jnp.bfloat16)
            return carry

        lax.fori_loop(0, groups, body, 0)
        far_copy(index).start()

    def finish_sum(index):
        far_copy(index).wait_recv()

        def body(group, squares):
            to = pl.ds(pl.multiple_of(group * 2 * SUB, 2 * SUB), 2 * SUB)
            own = keep[index][0, to, :].astype(jnp.float32) + near[index][0, to, :].astype(jnp.float32)
            own = own + far[index][to, :].astype(jnp.float32)
            keep[index][0, to, :] = own.astype(jnp.bfloat16)
            return squares + own * own

        start = jnp.zeros((2 * SUB, cuts[index]), jnp.float32)
        squares = lax.fori_loop(0, groups, body, start)
        return (
            jnp.sum(squares[:SUB], axis=0, keepdims=True),
            jnp.sum(squares[SUB:], axis=0, keepdims=True),
        )

    def send_map(index, weights, squares):
        product = lax.dot_general(
            unit_rows[...], weights, (((0,), (0,)), ((), ())), preferred_element_type=jnp.float32
        ).astype(jnp.bfloat16)
        share = g_send[index].shape[1]
        for goal in range(n):
            g_send[index][goal] = product[goal * share:(goal + 1) * share]
        q_send[index][0] = squares[0]
        q_send[index][1] = squares[1]

        def act(step):
            for copy in map_copies(index, step):
                copy.start()

        each_peer(act)

    def finish_map(index):
        def act(step):
            for copy in map_copies(index, step):
                copy.wait_recv()

        each_peer(act)
        product = g_send[index][me].astype(jnp.float32)
        squares = q_send[index][(me * 2) // n]
        for step in range(1, n):
            product = product + g_recv[index][step].astype(jnp.float32)
            squares = squares + q_recv[index][step]
        scaled = product * (1.0 / (EPS + jnp.sqrt(squares)))
        k_out[index][me] = scaled.astype(jnp.bfloat16)
        each_peer(lambda step: map_spread(index, step).start())

    def unit_in_rows(values):
        lane = lax.broadcasted_iota(jnp.int32, values.shape, 1)
        left = jnp.where(lane < LANES // 2, values, 0.0)
        norm = jnp.sqrt(jnp.sum(left * left, axis=1, keepdims=True))
        return left / (EPS + norm)

    def start_aux():
        squares = finish_sum(0)
        own = keep[0][0, :, 0:LANES]
        aux_all[me] = own
        each_peer(lambda step: aux_copy(step).start())
        unit = unit_in_rows(own.astype(jnp.float32))
        unit = unit + pltpu.roll(unit, LANES // 2, 1)
        row = lax.broadcasted_iota(jnp.int32, unit.shape, 0)
        lane = lax.broadcasted_iota(jnp.int32, unit.shape, 1)
        same = lax.rem(row, 2 * SUB) // SUB == lane // (LANES // 2)
        unit_rows[...] = jnp.where(same, unit, 0.0).astype(jnp.bfloat16)
        rest = keep[0][0, :, LANES:]
        proj_width = proj_w.shape[1] - LANES
        proj_w[:, proj_width:] = jnp.where(lane < LANES // 2, rest, jnp.zeros_like(rest))
        first = lax.broadcasted_iota(jnp.int32, (1, LANES), 1) < LANES // 2
        for profile in range(2):
            proj_sq[profile, :, proj_width:] = jnp.where(first, squares[profile][:, LANES:], 0.0)
        send_map(0, rest, [square[:, LANES:] for square in squares])

    def start_proj(index, offset):
        squares = finish_sum(index)
        proj_w[:, offset:offset + cuts[index]] = keep[index][0]
        for profile in range(2):
            proj_sq[profile, :, offset:offset + cuts[index]] = squares[profile]

    def out_maps():
        each_peer(lambda step: aux_copy(step).wait_recv())
        each_peer(lambda step: sq_copy(step).wait_recv())
        sums = proj_sq[...]
        for step in range(1, n):
            sums = sums + proj_sq_in[step]
        inverse = 1.0 / (EPS + jnp.sqrt(sums))
        values = aux_all[...].astype(jnp.float32).reshape(n * groups, 2 * SUB, LANES)
        results = []
        depth = n * real
        for profile in range(2):
            own = values[:, profile * SUB:(profile + 1) * SUB].reshape(n * groups * SUB, LANES)
            if real < groups * SUB:
                starts = range(0, n * groups * SUB, groups * SUB)
                own = jnp.concatenate([own[start:start + real] for start in starts], axis=0)
            norm = jnp.sqrt(jnp.sum(own * own, axis=0, keepdims=True))
            unit_out = (own / (EPS + norm)).astype(jnp.bfloat16)
            unit_in = unit_in_rows(own).astype(jnp.bfloat16)
            skip_out[profile] = lax.dot_general(
                unit_in, unit_out, (((0,), (0,)), ((), ())), preferred_element_type=jnp.float32
            )
            spare = jnp.zeros((proj_w.shape[1] - depth, LANES), jnp.bfloat16)
            tall = jnp.concatenate([unit_out, spare], axis=0)
            weights = (proj_w[...].astype(jnp.float32) * inverse[profile]).astype(jnp.bfloat16)
            results.append(jnp.dot(weights, tall, preferred_element_type=jnp.float32))
        row = lax.broadcasted_iota(jnp.int32, results[0].shape, 0)
        chosen = jnp.where(lax.rem(row, 2 * SUB) < SUB, results[0], results[1])
        m_out[me] = chosen.astype(jnp.bfloat16)
        each_peer(lambda step: m_copy(step).start())

    for copy in fetches(0):
        copy.start()
    for index in range(total):
        if index + 1 < total:
            for copy in fetches(index + 1):
                copy.start()
        for copy in fetches(index):
            copy.wait()
        contract(index)
        if index == 0:
            pl.semaphore_wait(barrier, n + 1)
        near_copy(index).start()
        if index >= 1:
            pass_on(index - 1)
    pass_on(total - 1)

    start_aux()
    offset = 0
    for index in range(1, proj_count + 1):
        start_proj(index, offset)
        offset += cuts[index]
    each_peer(lambda step: sq_copy(step).start())
    finish_map(0)

    def arrived(index):
        each_peer(lambda step: map_spread(index, step).wait_recv())

    def product_of(index, lane, profile):
        half = n // 2
        weights = k_out[index][pl.ds(profile * half, half), :, lane:lane + LANES]
        return jnp.dot(
            tokens[...], weights.reshape(LANES // 2, LANES), preferred_element_type=jnp.float32
        )

    def start_attention():
        each_peer(lambda step: m_copy(step).wait_recv())
        values = m_out[...].astype(jnp.float32).reshape(n * groups, 2 * SUB, LANES)
        for profile in range(2):
            own = values[:, profile * SUB:(profile + 1) * SUB].reshape(n * real, LANES)
            out_rows[profile] = own.astype(jnp.bfloat16)
            skip = jnp.dot(
                tokens[...].astype(jnp.float32), skip_out[profile, 0:LANES // 2],
                preferred_element_type=jnp.float32, precision=lax.Precision.HIGHEST,
            )
            feature[profile] = 0.7 * skip

    def attention(which):
        first, last = plan[which][0]
        heads = list(range(2 * first, 2 * last))
        count = proj.shape[2] // HEAD_DIM
        if which == len(plan) - 1:
            heads.append(count - 1)

        def body(profile, carry):
            found = {}
            row = lax.broadcasted_iota(jnp.int32, (LANES, LANES), 0) // HEAD_DIM
            lane = lax.broadcasted_iota(jnp.int32, (LANES, LANES), 1) // HEAD_DIM
            same = jnp.where(row == lane, 1.0 / HEAD_DIM, 0.0).astype(jnp.bfloat16)

            def unit(column):
                tile, start = column // LANES, column % LANES
                if tile not in found:
                    own = product_of(*places[tile], profile)
                    squares = own * own
                    high = squares.astype(jnp.bfloat16)
                    low = (squares - high.astype(jnp.float32)).astype(jnp.bfloat16)
                    mean = jnp.dot(high, same, preferred_element_type=jnp.float32)
                    mean = mean + jnp.dot(low, same, preferred_element_type=jnp.float32)
                    found[tile] = own * (1.0 / (EPS + jnp.sqrt(mean)))
                if tile == len(places) - 1:
                    start = LANES // 2
                return found[tile], start

            queries, keys, values, ends = [], [], [], []
            for head in heads:
                own, start = unit(head * HEAD_DIM)
                own = own[:, start:start + HEAD_DIM] * (1.0 / HEAD_DIM**0.5)
                queries.append(own.astype(jnp.bfloat16))
                own, start = unit((count + head) * HEAD_DIM)
                keys.append(own[:, start:start + HEAD_DIM].astype(jnp.bfloat16))
                own, start = unit((2 * count + head) * HEAD_DIM)
                side = lax.broadcasted_iota(jnp.int32, own.shape, 1) // HEAD_DIM
                own = jnp.where(side == start // HEAD_DIM, own, 1.0)
                values.append(own.astype(jnp.bfloat16))
                ends.append(start)
            expo = [
                jnp.exp(
                    lax.dot_general(
                        query, key, (((1,), (1,)), ((), ())), preferred_element_type=jnp.float32
                    )
                ).astype(jnp.bfloat16)
                for query, key in zip(queries, keys)
            ]
            sums = [
                jnp.dot(weight, value, preferred_element_type=jnp.float32)
                for weight, value in zip(expo, values)
            ]
            mixed = [
                (value * (1.0 / pltpu.roll(value, HEAD_DIM, 1)))[:, start:start + HEAD_DIM]
                for value, start in zip(sums, ends)
            ]
            added = jnp.zeros(feature.shape[1:], jnp.float32)
            for head, value in zip(heads, mixed):
                rows_of = out_rows[profile, head * HEAD_DIM:(head + 1) * HEAD_DIM, :]
                added = added + jnp.dot(
                    value.astype(jnp.bfloat16), rows_of, preferred_element_type=jnp.float32
                )
            feature[profile] = feature[profile] + 0.3 * added
            return carry

        lax.fori_loop(0, 2, body, 0)

    for index in range(1, maps):
        chunk = index + proj_count
        squares = finish_sum(chunk)
        send_map(index, keep[chunk][0], squares)
        if index == 1:
            out_maps()
            arrived(0)
        elif fused:
            if index == 2:
                start_attention()
            arrived(index - 1)
            attention(index - 2)
        finish_map(index)
    arrived(maps - 1)
    if fused:
        attention(maps - 2)
    else:
        for index in range(1, maps - 1):
            arrived(index)
        each_peer(lambda step: m_copy(step).wait_recv())
        feature[...] = jnp.zeros(feature.shape, feature.dtype)
    for index in range(total):
        near_copy(index).wait_send()
        far_copy(index).wait_send()

    def drain(step):
        for index in range(maps):
            for copy in map_copies(index, step):
                copy.wait_send()
            map_spread(index, step).wait_send()
        aux_copy(step).wait_send()
        sq_copy(step).wait_send()
        m_copy(step).wait_send()

    each_peer(drain)


def exchange_call(coeffs, aux, proj, qkv, tokens, n, real, main_proj, plan, fused):
    snaps, rows, _ = aux.shape
    groups = rows // SUB
    proj_cuts = cut(main_proj, 2)
    cuts = [aux.shape[2]] + proj_cuts
    cuts += [sum(last - first for first, last in parts) * LANES for parts in plan]
    total = len(cuts)
    map_cuts = [LANES] + cuts[1 + len(proj_cuts):]
    maps = len(map_cuts)
    both = 2 * rows
    share = LANES // n
    proj_wide = main_proj + LANES
    kind, wide = jnp.bfloat16, jnp.float32
    shapes = [jax.ShapeDtypeStruct((n, share, width), kind) for width in map_cuts]
    shapes += [
        jax.ShapeDtypeStruct((n, both, LANES), kind),
        jax.ShapeDtypeStruct((2, LANES, LANES), wide),
        jax.ShapeDtypeStruct((2, tokens.shape[0], LANES), wide),
    ]
    scratch = [pltpu.VMEM((2, snaps, rows, max(cuts)), wide)]
    for lead in ((2,), (2,), (2,), (), ()):
        scratch += [pltpu.VMEM(lead + (both, width), kind) for width in cuts]
    scratch += [pltpu.VMEM((n, share, width), kind) for width in map_cuts]
    scratch += [pltpu.VMEM((n, share, width), kind) for width in map_cuts]
    scratch += [pltpu.VMEM((2, 1, width), wide) for width in map_cuts]
    scratch += [pltpu.VMEM((n, 1, width), wide) for width in map_cuts]
    scratch += [
        pltpu.VMEM((n, both, LANES), kind),
        pltpu.VMEM((both, proj_wide), kind),
        pltpu.VMEM((2, 1, proj_wide), wide),
        pltpu.VMEM((n, 2, 1, proj_wide), wide),
        pltpu.VMEM((both, LANES), kind),
        pltpu.VMEM((2, n * real, LANES), kind),
        pltpu.VMEM((coeffs.shape[1], snaps, SUB, LANES), wide),
        pltpu.SemaphoreType.DMA((2, 3)),
        pltpu.SemaphoreType.DMA((2, total)),
        pltpu.SemaphoreType.DMA((2, total)),
        pltpu.SemaphoreType.DMA((2, maps, 3, n)),
        pltpu.SemaphoreType.DMA((2, n)),
        pltpu.SemaphoreType.DMA((2, n)),
        pltpu.SemaphoreType.DMA((2, n)),
    ]
    hbm = pl.BlockSpec(memory_space=pl.ANY)
    return pl.pallas_call(
        functools.partial(
            exchange_kernel, plan, tuple(cuts), len(proj_cuts), n, groups, real, fused
        ),
        out_shape=shapes,
        in_specs=[
            pl.BlockSpec(memory_space=pltpu.SMEM), hbm, hbm, hbm,
            pl.BlockSpec(memory_space=pltpu.VMEM),
        ],
        out_specs=[pl.BlockSpec(memory_space=pltpu.VMEM)] * len(shapes),
        scratch_shapes=scratch,
        compiler_params=pltpu.CompilerParams(
            collective_id=0, has_side_effects=True, vmem_limit_bytes=60 * 2**20
        ),
    )(coeffs, aux, proj, qkv, tokens)


def shards(snap_in, snap_qkv, snap_proj, snap_out, coeffs, latent, levels):
    owned = PROF // lax.axis_size("snap")
    n = lax.axis_size("param")
    width = snap_proj.shape[2]
    rows = snap_qkv.shape[1]
    main_proj = width // LANES * LANES
    main_qkv = snap_qkv.shape[2] // LANES * LANES
    aux = jnp.concatenate(
        [snap_in.transpose(0, 2, 1), snap_out, snap_proj[:, :, main_proj:], snap_qkv[:, :, main_qkv:]],
        axis=2,
    )
    main = [snap_proj, snap_qkv]
    spare = -rows % SUB
    if spare:
        aux, *main = [jnp.pad(x, ((0, 0), (0, spare), (0, 0))) for x in [aux] + main]
    plan = head_plan(width // LANES)
    share = owned * snap_in.shape[1] // n
    fused = rows % SUB == 0 and share % (2 * SUB) == 0 and latent.shape[0] == 1
    tokens, c_skip, c_out = prepare(latent, levels)
    *maps, out_map, skip_map, feature = exchange_call(
        coeffs, aux, main[0], main[1], tokens, n, rows, main_proj, plan, fused
    )
    half = LANES // 2
    if fused:
        feature = feature[:, :, half:] / jnp.sqrt(0.58)
        return jnp.stack([finish(feature[p], latent, c_skip, c_out) for p in range(owned)])
    maps = [part.reshape(owned, -1, part.shape[2]) for part in maps]
    places = tile_places(plan)
    tiles = []
    for tile in range(len(places) - 1):
        index, lane = places[tile]
        tiles.append(maps[index][:, :, lane:lane + LANES])
    qkv_map = jnp.concatenate(tiles + [maps[0][:, :, half:]], axis=2)
    out_map = out_map.reshape(n, -1, owned, SUB, LANES)[..., half:]
    out_map = out_map.transpose(2, 0, 1, 3, 4).reshape(owned, n, -1, half)[:, :, :rows]
    out_map = out_map.reshape(owned, n * rows, half)
    skip_map = skip_map[:, :half, half:]
    results = []
    for profile in range(owned):
        feature = attend(tokens, qkv_map[profile], out_map[profile], skip_map[profile])
        results.append(finish(feature, latent, c_skip, c_out))
    return jnp.stack(results)


def solution(mesh):
    in_specs = (
        P("snap", None, "param"),
        P("snap", "param", None),
        P("snap", "param", None),
        P("snap", "param", None),
        P("snap", None),
        P("param", None, None),
        P("param"),
    )
    out_specs = P("snap", "param", None, None)
    return jax.shard_map(shards, mesh=mesh, in_specs=in_specs, out_specs=out_specs, check_vma=False)
```
